256 devices in a mesh: tm: 64 (over y, z, core), obs: 4 (over x).
Axes of the slice: x: 4, y: 4, z: 8, core: 2. Of those that a mesh axis runs over, the one named last changes fastest.
Arguments:
- weights: bfloat16 [64, 16384, 128], P('tm', 'obs'), may hold values from -0.0546875 to 0.0546875
- tile_of: int32 [64, 16384], P('tm', 'obs'), may hold values from 0 to 31
- obs_prec: float32 [64, 16384], P('tm', 'obs'), may hold values from 0.01 to 0.4
- obs_value: float32 [64, 16384], P('tm', 'obs'), may hold values from -6 to 6
- node_kappa: float32 [4096], P('obs'), may hold values from 0.5 to 4
- rate: float32 [64, 32], P('tm', 'obs'), may hold values from 0.94 to 0.99
Outputs:
- post_mean: float32 [64, 4096], P('tm', 'obs')
The draws below stay inside these ranges and needn't reach their ends.
Inputs may be any that keep to these rules, and one draw needn't show every extreme that they name: `tile_of`: every entry names one of the 32 tiles.
All inputs are finite; a program needn't handle non-finite values.
Results may differ from the reference program's by a relative error of at most 0.00035.
Values may be sent and summed in bfloat16 or wider, within the bound.
A program may use at most 64 MiB of HBM per device.

```python
import math
import jax
import jax.numpy as jnp
from jax import lax

NODES = 4096
TILES = 32
TSTEPS = 64
OBS = 16384


def plant(values, rng, least, high):
    spot = [jax.random.randint(jax.random.fold_in(rng, axis), (), 0, length) for axis, length in enumerate(values.shape)]
    longest = values.shape.index(max(values.shape))
    beside = spot[:longest] + [(spot[longest] + 1) % values.shape[longest]] + spot[longest + 1:]
    return values.at[tuple(spot)].set(least).at[tuple(beside)].set(high)


def levels(stream_key, extent, cuts, smallest, top_value):
    def one(dim, shards_of):
        steps = jax.random.uniform(jax.random.fold_in(jax.random.fold_in(stream_key, 6), dim), (shards_of,), jnp.float32, smallest / len(cuts), top_value / len(cuts))
        return jnp.repeat(jnp.exp(steps), extent[dim] // shards_of).reshape((-1,) + (1,) * (len(extent) - dim - 1))

    level = one(*cuts[0])
    for cut in cuts[1:]:
        level = level * one(*cut)
    return level


def gaussian(rng, shape, deviation, bound, cuts=(), kind=jnp.bfloat16):
    entries = deviation * jax.random.normal(rng, shape, jnp.float32)
    if cuts:
        entries = entries * levels(rng, shape, cuts, -0.22, 0.18)
    return jnp.clip(entries, -bound, bound).astype(kind)


def setup_inputs(seed: int = 0) -> dict:
    arg_keys = jax.random.split(jax.random.key(seed), 7)
    weights = gaussian(arg_keys[0], (TSTEPS, OBS, 128), 12800 ** -0.5, 0.0546875, ((0, 64), (1, 4)))
    tile_of = plant(jax.random.randint(arg_keys[1], (TSTEPS, OBS), 0, TILES), jax.random.fold_in(arg_keys[1], 1), 0, TILES - 1).astype(jnp.int32)
    obs_prec = jnp.clip(jnp.exp(math.log(0.4) - 3.6888795 * jax.random.uniform(arg_keys[2], (TSTEPS, OBS), jnp.float32) ** levels(arg_keys[2], (TSTEPS, OBS), ((0, 64), (1, 4)), -0.2, 0.2)), 0.01, 0.4)
    obs_value = gaussian(arg_keys[3], (TSTEPS, OBS), 1.0, 6.0, ((0, 64), (1, 4)), jnp.float32)
    node_kappa = jnp.clip(jnp.exp(math.log(4.0) - 2.0794415 * jax.random.uniform(arg_keys[4], (NODES,), jnp.float32) ** levels(arg_keys[4], (NODES,), ((0, 4),), -0.2, 0.2)), 0.5, 4.0)
    rate = jnp.clip(0.94 + 0.050000012 * jax.random.uniform(arg_keys[5], (TSTEPS, TILES), jnp.float32) ** levels(arg_keys[5], (TSTEPS, TILES), ((0, 64), (1, 4)), -0.2, 0.2), 0.94, 0.99)
    return {"weights": weights, "tile_of": tile_of, "obs_prec": obs_prec, "obs_value": obs_value, "node_kappa": node_kappa, "rate": rate}


def spatial_prior(kappa):
    kappa_tiles = kappa.reshape(-1, 128)
    position = jnp.arange(128)
    degree = jnp.where((position == 0) | (position == 127), 1.0, 2.0).astype(jnp.float32)
    identity = jnp.eye(128, dtype=jnp.float32)
    neighbour = (jnp.abs(position[:, None] - position[None, :]) == 1).astype(jnp.float32)
    return (kappa_tiles + degree)[:, :, None] * identity - neighbour

def pairwise(left, right):
    return jnp.einsum('kab,kac->kbc', left, right, precision=lax.Precision.HIGHEST)

def lower_solve(factor, target):
    return jax.scipy.linalg.solve_triangular(factor, target, lower=True)

def observation_terms(weights_step, tile_ids, prec_step, value_step):
    block = math.gcd(OBS, 1024)
    widened = weights_step.astype(jnp.float32)
    rounded = (prec_step[:, None] * widened).astype(jnp.bfloat16)
    rounded = lax.optimization_barrier(rounded).astype(jnp.float32)
    right_side = jax.ops.segment_sum((prec_step * value_step)[:, None] * widened, tile_ids, num_segments=TILES)

    def add_block(total, pieces):
        part_weights, part_scaled, part_ids = pieces
        outer = part_scaled[:, :, None] * part_weights[:, None, :]
        return (total + jax.ops.segment_sum(outer, part_ids, num_segments=TILES), None)
    matrix, _ = lax.scan(add_block, jnp.zeros((TILES, 128, 128), jnp.float32), (widened.reshape(-1, block, 128), rounded.reshape(-1, block, 128), tile_ids.reshape(-1, block)))
    return (matrix, right_side)

def reference(weights, tile_of, obs_prec, obs_value, node_kappa, rate):
    prior = spatial_prior(node_kappa)
    rate_next = jnp.concatenate([rate[1:], jnp.zeros((1, TILES), jnp.float32)], axis=0)
    first_step = (jnp.arange(TSTEPS) == 0)[:, None]
    leading = jnp.where(first_step, 1.0 - rate * rate, jnp.ones_like(rate))
    coupling_rate = jnp.where(first_step, jnp.zeros_like(rate), rate)
    identity = jnp.broadcast_to(jnp.eye(128, dtype=jnp.float32), (TILES, 128, 128))

    def forward(carry, inputs):
        factor_prev, vector_prev = carry
        weights_step, tile_ids, prec_step, value_step, lead_step, next_step, couple_step = inputs
        matrix, right_side = observation_terms(weights_step, tile_ids, prec_step, value_step)
        diagonal_block = (lead_step + next_step * next_step)[:, None, None] * prior + matrix
        coupling = -couple_step[:, None, None] * prior
        gain = lower_solve(factor_prev, coupling)
        schur = diagonal_block - pairwise(gain, gain)
        factor = jnp.linalg.cholesky(schur)
        carried = pairwise(gain, vector_prev[:, :, None])[:, :, 0]
        vector = lower_solve(factor, (right_side - carried)[:, :, None])[:, :, 0]
        return ((factor, vector), (factor, gain, vector))
    start = (identity, jnp.zeros((TILES, 128), jnp.float32))
    _, (factors, gains, vectors) = lax.scan(forward, start, (weights, tile_of, obs_prec, obs_value, leading, rate_next, coupling_rate))
    gains_next = jnp.concatenate([gains[1:], jnp.zeros((1, TILES, 128, 128), jnp.float32)], axis=0)

    def backward(later, inputs):
        factor, gain_next, vector = inputs
        target = vector - jnp.einsum('kab,kb->ka', gain_next, later, precision=lax.Precision.HIGHEST)
        current = jax.scipy.linalg.solve_triangular(factor, target[:, :, None], lower=True, trans=1)[:, :, 0]
        return (current, current)
    _, states = lax.scan(backward, jnp.zeros((TILES, 128), jnp.float32), (factors, gains_next, vectors), reverse=True)
    return states.reshape(TSTEPS, NODES)
```

```python
import functools

import jax
import jax.numpy as jnp
from jax import lax
from jax.experimental import pallas as pl
from jax.experimental.pallas import tpu as pltpu
from jax.sharding import PartitionSpec as P

F32 = jnp.float32
BF16 = jnp.bfloat16
N = 128
SPAN = 8
MESH = pl.DeviceIdType.MESH


def dot(left, right, dims=((1,), (0,))):
    return lax.dot_general(
        left, right, (dims, ((), ())), precision=lax.Precision.HIGHEST, preferred_element_type=F32
    )


def gram_kernel(rows_ref, label_ref, prec_ref, value_ref, gram_ref, side_ref, left_ref, *, pairs):
    step = pl.program_id(0)
    turned = rows_ref[...].astype(F32).T
    prec = prec_ref[...]
    label = label_ref[...]
    pair = lax.shift_right_logical(label, 1)
    odd = lax.bitwise_and(label, 1)
    scaled = (turned * prec).astype(BF16).astype(F32)
    both = jnp.concatenate(
        [jnp.where(odd == 0, turned, 0.0).astype(BF16), jnp.where(odd == 1, turned, 0.0).astype(BF16)], axis=0
    )
    for p in range(pairs):
        left_ref[pl.ds(p * N, N), :] = jnp.where(pair == p, scaled, 0.0).astype(BF16)
    part = prec * value_ref[...]
    match = lax.broadcasted_iota(jnp.int32, (pairs, part.shape[1]), 0) == pair
    pieces = []
    for _ in range(3):
        top = part.astype(BF16).astype(F32)
        pieces.append(jnp.where(match, top, 0.0).astype(BF16))
        part = part - top
    side = lax.dot_general(
        jnp.concatenate(pieces, axis=0), both, (((1,), (1,)), ((), ())), preferred_element_type=F32
    )
    side = side[:pairs] + side[pairs:2 * pairs] + side[2 * pairs:]

    @pl.when(step == 0)
    def _():
        gram_ref[...] = jnp.zeros_like(gram_ref)
        side_ref[...] = jnp.zeros_like(side_ref)

    side_ref[...] += side
    total = lax.dot_general(
        left_ref[...], both, (((1,), (1,)), ((), ())), preferred_element_type=F32
    )
    for p in range(pairs):
        gram_ref[2 * p] += total[p * N:(p + 1) * N, :N]
        gram_ref[2 * p + 1] += total[p * N:(p + 1) * N, N:]


def tile_terms(rows, label, prec, value, count):
    total_rows = rows.shape[0]
    block = min(1024, total_rows)
    pairs = count // 2
    row = lambda a: a.reshape(1, total_rows)
    flat = pl.BlockSpec((1, block), lambda i: (0, i))
    gram, side = pl.pallas_call(
        functools.partial(gram_kernel, pairs=pairs),
        grid=(total_rows // block,),
        in_specs=[pl.BlockSpec((block, N), lambda i: (i, 0)), flat, flat, flat],
        out_specs=[
            pl.BlockSpec((count, N, N), lambda i: (0, 0, 0)),
            pl.BlockSpec((pairs, 2 * N), lambda i: (0, 0)),
        ],
        out_shape=[
            jax.ShapeDtypeStruct((count, N, N), F32),
            jax.ShapeDtypeStruct((pairs, 2 * N), F32),
        ],
        scratch_shapes=[pltpu.VMEM((pairs * N, block), BF16)],
        compiler_params=pltpu.CompilerParams(vmem_limit_bytes=48 * 2**20),
        name="gram",
    )(rows, row(label), row(prec), row(value))
    return gram, side.reshape(count, N)


def invert(work, batch):
    lane = lax.broadcasted_iota(jnp.int32, (1, N), 1)
    height = lax.broadcasted_iota(jnp.int32, (8, 1), 0)

    def block(_, carry):
        mats = [work[b] for b in range(batch)]
        for j in range(8):
            at = lane == j
            here = height == j
            for b in range(batch):
                m = mats[b]
                row = m[j:j + 1, :]
                scale = 1.0 / row[:, j:j + 1]
                row = jnp.where(at, scale, row * scale)
                column = m[:, j:j + 1]
                m = jnp.where(at, 0.0, m) - column * row
                mats[b] = jnp.concatenate([jnp.where(here, row, m[:8]), m[8:]], axis=0)
        for b in range(batch):
            m = pltpu.roll(mats[b], N - 8, 1)
            work[b] = jnp.concatenate([m[8:], m[:8]], axis=0)
        return carry

    lax.fori_loop(0, N // 8, block, 0)


def pad_rows(row):
    return jnp.broadcast_to(row, (8, N))


def solve_kernel(
    gram_ref, side_ref, kappa_ref, rate_ref, out_ref,
    work, keep, spread2, spread4, held, coupling, send, recv, send_x, recv_x, zs,
    send_sem, recv_sem, x_sems, *, chunks, owner,
):
    me = lax.axis_index("tm")
    chunk, tile = owner.chunk_of(me), owner.tile_of(me)
    levels = chunks.bit_length() - 1
    strides = [2 ** i for i in range(levels)]

    def device(other):
        return (owner.device(other, tile), lax.axis_index("obs"))

    stage_list = []
    for d in sorted(set([1] + strides)):
        stage_list += [-d, d]

    def exists(step):
        return jnp.logical_and(chunk + step >= 0, chunk + step < chunks)

    recv[...] = jnp.zeros_like(recv)
    recv_x[...] = jnp.zeros_like(recv_x)

    barrier = pltpu.get_barrier_semaphore()
    partners = 0
    for step in stage_list:
        @pl.when(exists(step))
        def _():
            pl.semaphore_signal(barrier, inc=1, device_id=device(chunk + step), device_id_type=MESH)
        partners = partners + exists(step).astype(jnp.int32)

    row_id = lax.broadcasted_iota(jnp.int32, (N, N), 0)
    lane_id = lax.broadcasted_iota(jnp.int32, (N, N), 1)
    end = jnp.logical_or(lane_id == 0, lane_id == N - 1)
    degree = jnp.where(end, 1.0, 2.0)
    prior = jnp.where(
        row_id == lane_id, kappa_ref[...] + degree,
        jnp.where(jnp.abs(row_id - lane_id) == 1, -1.0, 0.0),
    )
    weight_row = kappa_ref[...] + degree[:1]
    weight_column = jnp.sum(jnp.where(row_id == lane_id, prior, 0.0), axis=1, keepdims=True)

    def prior_left(m):
        up = jnp.where(row_id == 0, 0.0, pltpu.roll(m, 1, 0))
        down = jnp.where(row_id == N - 1, 0.0, pltpu.roll(m, N - 1, 0))
        return weight_column * m - up - down

    def prior_right(m):
        lanes = lax.broadcasted_iota(jnp.int32, m.shape, 1)
        up = jnp.where(lanes == 0, 0.0, pltpu.roll(m, 1, 1))
        down = jnp.where(lanes == N - 1, 0.0, pltpu.roll(m, N - 1, 1))
        return weight_row * m - up - down

    rates = [rate_ref[i] for i in range(SPAN + 1)]
    first = chunk == 0

    def diagonal(i):
        lead = 1.0
        if i == 0:
            lead = jnp.where(first, 1.0 - rates[0] * rates[0], 1.0)
        g = gram_ref[i]
        return (lead + rates[i + 1] * rates[i + 1]) * prior + 0.5 * (g + g.T)

    def side(i):
        return pad_rows(side_ref[i:i + 1, :])

    for b in range(4):
        work[b] = diagonal(2 * b + 1)
    invert(work, 4)
    sides = {i: side(i) for i in range(0, SPAN, 2)}
    after_side = jnp.zeros((8, N), F32)
    for b in range(4):
        i = 2 * b + 1
        inverse = work[b]
        keep[b] = inverse
        middle = prior_right(prior_left(inverse))
        z = dot(side(i), inverse)
        zs[i] = z
        pz = prior_right(z)
        low, high = rates[i], rates[i + 1]
        held[2 * b] = (diagonal(2 * b) if b == 0 else held[2 * b]) - (low * low) * middle
        coupling[b] = (-low * high) * middle
        sides[i - 1] = sides[i - 1] + low * pz
        if b < 3:
            held[2 * b + 2] = diagonal(2 * b + 2) - (high * high) * middle
            sides[i + 1] = sides[i + 1] + high * pz
        else:
            send[0, 0, 0:N, :] = (high * high) * middle
            after_side = after_side - high * pz

    work[0] = held[2]
    work[1] = held[6]
    invert(work, 2)
    for b, i in ((0, 2), (1, 6)):
        wide = jnp.concatenate([coupling[2 * b], coupling[2 * b + 1]], axis=1)
        tall = jnp.concatenate([coupling[2 * b], coupling[2 * b + 1]], axis=0)
        inverse = work[b]
        x = dot(inverse, wide)
        spread2[b] = x
        z = dot(sides[i], inverse)
        zs[i] = z
        vec = dot(z, wide)
        s = dot(tall, x)
        held[i - 2] = held[i - 2] - s[:N, :N]
        sides[i - 2] = sides[i - 2] - vec[:, :N]
        if b == 0:
            held[4] = held[4] - s[N:, N:]
            sides[4] = sides[4] - vec[:, N:]
            coupling[0] = -s[N:, :N]
            coupling[1] = -s[:N, N:]
        else:
            send[0, 0, 0:N, :] += s[N:, N:]
            after_side = after_side + vec[:, N:]
            coupling[2] = -s[:N, N:]
            coupling[3] = -s[N:, :N]

    work[0] = held[4]
    invert(work, 1)
    wide = jnp.concatenate([coupling[0], coupling[2]], axis=1)
    tall = jnp.concatenate([coupling[1], coupling[3]], axis=0)
    inverse = work[0]
    x = dot(inverse, wide)
    spread4[...] = x
    z = dot(sides[4], inverse)
    zs[4] = z
    vec = dot(z, wide)
    s = dot(tall, x)
    right = -s[:N, N:]
    send[0, 0, 0:N, :] += s[N:, N:]
    send[0, 0, N:2 * N, :] = s[N:, :N]
    send[0, 0, 2 * N:, :] = after_side + vec[:, N:]

    pl.semaphore_wait(barrier, partners)

    def copy(stage, way, step):
        return pltpu.make_async_remote_copy(
            src_ref=send.at[stage, way], dst_ref=recv.at[stage, way],
            send_sem=send_sem.at[stage, way], recv_sem=recv_sem.at[stage, way],
            device_id=device(chunk + step), device_id_type=MESH,
        )

    def start(stage, way, step):
        @pl.when(exists(step))
        def _():
            copy(stage, way, step).start()

    def arrive(stage, way, step):
        @pl.when(exists(-step))
        def _():
            copy(stage, way, step).wait_recv()

    start(0, 0, 1)
    diag = held[0] - s[:N, :N]
    vector = sides[0] - vec[:, :N]
    arrive(0, 0, 1)
    diag = diag - recv[0, 0, 0:N, :]
    left = -recv[0, 0, N:2 * N, :]
    vector = vector - recv[0, 0, 2 * N:, :]

    for stage, stride in enumerate(strides, 1):
        work[0] = diag
        invert(work, 1)
        inverse = work[0]
        wide = jnp.concatenate([left, right], axis=1)
        tall = jnp.concatenate([left.T, right.T], axis=0)
        x = dot(inverse, wide)
        z = dot(vector, inverse)
        vec = dot(z, wide)
        s = dot(tall, x)
        send[stage, 0, 0:N, :] = s[N:, N:]
        send[stage, 0, N:2 * N, :] = s[N:, :N]
        send[stage, 0, 2 * N:, :] = vec[:, N:]
        start(stage, 0, stride)
        send[stage, 1, 0:N, :] = s[:N, :N]
        send[stage, 1, N:2 * N, :] = s[:N, N:]
        send[stage, 1, 2 * N:, :] = vec[:, :N]
        start(stage, 1, -stride)
        arrive(stage, 0, stride)
        arrive(stage, 1, -stride)
        diag = diag - recv[stage, 0, 0:N, :] - recv[stage, 1, 0:N, :]
        left = -recv[stage, 0, N:2 * N, :]
        right = -recv[stage, 1, N:2 * N, :]
        vector = vector - recv[stage, 0, 2 * N:, :] - recv[stage, 1, 2 * N:, :]

    work[0] = diag
    invert(work, 1)
    x0 = dot(vector, work[0])
    send_x[...] = x0

    def copy_x():
        return pltpu.make_async_remote_copy(
            src_ref=send_x, dst_ref=recv_x, send_sem=x_sems.at[0], recv_sem=x_sems.at[1],
            device_id=device(chunk - 1), device_id_type=MESH,
        )

    @pl.when(exists(-1))
    def _():
        copy_x().start()

    @pl.when(exists(1))
    def _():
        copy_x().wait_recv()

    x8 = recv_x[...]
    found = {0: x0, 8: x8}
    last = ((1,), (1,))
    found[4] = zs[4] - dot(jnp.concatenate([x0, x8], axis=1), spread4[...], last)
    for b, i in ((0, 2), (1, 6)):
        found[i] = zs[i] - dot(jnp.concatenate([found[i - 2], found[i + 2]], axis=1), spread2[b], last)
    for b in range(4):
        i = 2 * b + 1
        mixed = rates[i] * found[i - 1] + rates[i + 1] * found[i + 1]
        found[i] = zs[i] + dot(prior_right(mixed), keep[b])
    out_ref[...] = jnp.concatenate([found[i][:1] for i in range(SPAN)], axis=0)

    @pl.when(exists(-1))
    def _():
        copy_x().wait_send()

    @pl.when(exists(1))
    def _():
        copy(0, 0, 1).wait_send()

    for stage, stride in enumerate(strides, 1):
        @pl.when(exists(stride))
        def _():
            copy(stage, 0, stride).wait_send()

        @pl.when(exists(-stride))
        def _():
            copy(stage, 1, -stride).wait_send()


class Consecutive:
    def chunk_of(self, me):
        return me // SPAN

    def tile_of(self, me):
        return me % SPAN

    def device(self, chunk, tile):
        return chunk * SPAN + tile


def solve(gram, side, kappa, rates, chunks):
    stages = chunks.bit_length()
    vmem = pl.BlockSpec(memory_space=pltpu.VMEM)
    return pl.pallas_call(
        functools.partial(solve_kernel, chunks=chunks, owner=Consecutive()),
        in_specs=[vmem, vmem, vmem, pl.BlockSpec(memory_space=pltpu.SMEM)],
        out_specs=vmem,
        out_shape=jax.ShapeDtypeStruct((SPAN, N), F32),
        scratch_shapes=[
            pltpu.VMEM((4, N, N), F32),
            pltpu.VMEM((4, N, N), F32),
            pltpu.VMEM((2, N, 2 * N), F32),
            pltpu.VMEM((N, 2 * N), F32),
            pltpu.VMEM((SPAN, N, N), F32),
            pltpu.VMEM((4, N, N), F32),
            pltpu.VMEM((stages, 2, 2 * N + 8, N), F32),
            pltpu.VMEM((stages, 2, 2 * N + 8, N), F32),
            pltpu.VMEM((8, N), F32),
            pltpu.VMEM((8, N), F32),
            pltpu.VMEM((SPAN, 8, N), F32),
            pltpu.SemaphoreType.DMA((stages, 2)),
            pltpu.SemaphoreType.DMA((stages, 2)),
            pltpu.SemaphoreType.DMA((2,)),
        ],
        compiler_params=pltpu.CompilerParams(
            collective_id=0, has_side_effects=True, vmem_limit_bytes=48 * 2**20
        ),
        name="solve",
    )(gram, side, kappa, rates)


def on_device(weights, tile_of, obs_prec, obs_value, node_kappa, rate):
    owned = node_kappa.shape[0] // N
    peers = lax.axis_size("obs")
    steps = lax.axis_size("tm")
    chunks = steps // SPAN
    me = lax.axis_index("tm")
    all_rates = lax.all_gather(rate[0], "tm")
    gram, side = tile_terms(weights[0], tile_of[0], obs_prec[0], obs_value[0], owned * peers)
    totals = lax.psum_scatter(
        jnp.concatenate([gram, side[:, None, :]], axis=1), "obs", scatter_dimension=0, tiled=True
    )
    groups = [[SPAN * c + k for k in range(SPAN)] for c in range(chunks)]
    mine = lax.all_to_all(totals, "tm", 0, 0, axis_index_groups=groups, tiled=True)
    chunk, tile = me // SPAN, me % SPAN
    kappa = lax.dynamic_slice(node_kappa.reshape(owned, N), (tile, 0), (1, N))
    padded = jnp.concatenate([all_rates, jnp.zeros((SPAN, owned), F32)], axis=0)
    rates = lax.dynamic_slice(padded, (chunk * SPAN, tile), (2 * SPAN, 1))[:, 0]
    states = solve(mine[:, :N], mine[:, N], kappa, rates, chunks)
    back = lax.all_to_all(states, "tm", 0, 0, axis_index_groups=groups, tiled=True)
    return back.reshape(1, owned * N)


def solution(mesh):
    placed = (
        P("tm", "obs", None),
        P("tm", "obs"),
        P("tm", "obs"),
        P("tm", "obs"),
        P("obs"),
        P("tm", "obs"),
    )
    return jax.shard_map(
        on_device, mesh=mesh, in_specs=placed, out_specs=P("tm", "obs"), check_vma=False
    )
```

```python
import functools

import jax
import jax.numpy as jnp
from jax import lax
from jax.experimental import pallas as pl
from jax.experimental.pallas import tpu as pltpu
from jax.sharding import PartitionSpec as P

F32 = jnp.float32
BF16 = jnp.bfloat16
N = 128
SPAN = 8
MESH = pl.DeviceIdType.MESH


def dot(left, right, dims=((1,), (0,))):
    return lax.dot_general(
        left, right, (dims, ((), ())), precision=lax.Precision.HIGHEST, preferred_element_type=F32
    )


def gram_kernel(rows_ref, label_ref, prec_ref, value_ref, gram_ref, side_ref, left_ref, *, pairs):
    step = pl.program_id(0)
    turned = rows_ref[...].astype(F32).T
    prec = prec_ref[...]
    label = label_ref[...]
    pair = lax.shift_right_logical(label, 1)
    odd = lax.bitwise_and(label, 1)
    scaled = (turned * prec).astype(BF16).astype(F32)
    both = jnp.concatenate(
        [jnp.where(odd == 0, turned, 0.0).astype(BF16), jnp.where(odd == 1, turned, 0.0).astype(BF16)], axis=0
    )
    for p in range(pairs):
        left_ref[pl.ds(p * N, N), :] = jnp.where(pair == p, scaled, 0.0).astype(BF16)
    part = prec * value_ref[...]
    match = lax.broadcasted_iota(jnp.int32, (pairs, part.shape[1]), 0) == pair
    pieces = []
    for _ in range(3):
        top = part.astype(BF16).astype(F32)
        pieces.append(jnp.where(match, top, 0.0).astype(BF16))
        part = part - top
    side = lax.dot_general(
        jnp.concatenate(pieces, axis=0), both, (((1,), (1,)), ((), ())), preferred_element_type=F32
    )
    side = side[:pairs] + side[pairs:2 * pairs] + side[2 * pairs:]

    @pl.when(step == 0)
    def _():
        gram_ref[...] = jnp.zeros_like(gram_ref)
        side_ref[...] = jnp.zeros_like(side_ref)

    side_ref[...] += side
    total = lax.dot_general(
        left_ref[...], both, (((1,), (1,)), ((), ())), preferred_element_type=F32
    )
    for p in range(pairs):
        gram_ref[2 * p] += total[p * N:(p + 1) * N, :N]
        gram_ref[2 * p + 1] += total[p * N:(p + 1) * N, N:]


def tile_terms(rows, label, prec, value, count):
    total_rows = rows.shape[0]
    block = min(1024, total_rows)
    pairs = count // 2
    row = lambda a: a.reshape(1, total_rows)
    flat = pl.BlockSpec((1, block), lambda i: (0, i))
    gram, side = pl.pallas_call(
        functools.partial(gram_kernel, pairs=pairs),
        grid=(total_rows // block,),
        in_specs=[pl.BlockSpec((block, N), lambda i: (i, 0)), flat, flat, flat],
        out_specs=[
            pl.BlockSpec((count, N, N), lambda i: (0, 0, 0)),
            pl.BlockSpec((pairs, 2 * N), lambda i: (0, 0)),
        ],
        out_shape=[
            jax.ShapeDtypeStruct((count, N, N), F32),
            jax.ShapeDtypeStruct((pairs, 2 * N), F32),
        ],
        scratch_shapes=[pltpu.VMEM((pairs * N, block), BF16)],
        compiler_params=pltpu.CompilerParams(vmem_limit_bytes=48 * 2**20),
        name="gram",
    )(rows, row(label), row(prec), row(value))
    return gram, side.reshape(count, N)


def reciprocal(x):
    r = pltpu.reciprocal(x, approx=True)
    r = r * (2.0 - x * r)
    return r * (2.0 - x * r)
def full(x):
    return jnp.broadcast_to(x, (8, N))
def invert(work, batch):
    panel = 16
    slabs = panel // 8
    lane = lax.broadcasted_iota(jnp.int32, (8, N), 1)
    sub = lax.broadcasted_iota(jnp.int32, (8, N), 0)
    at = lambda x, s: full(x[s:s + 1, :])

    def load(first, b):
        return [work[b, pl.ds(pl.multiple_of(first + 8 * v, 8), 8), :] for v in range(slabs)]

    def spread(mats, first):
        picks = [jnp.full((8, N), k, jnp.int32) + first for k in range(panel)]
        return [
            [jnp.take_along_axis(m, pick, axis=1, mode="promise_in_bounds") for m in mats] for pick in picks
        ]

    def step(index, carry):
        first = pl.multiple_of(index * panel, panel)
        rows = [load(first, b) for b in range(batch)]
        columns = [spread(rows[b], first) for b in range(batch)]
        place = lane - first
        for j0 in range(0, panel, 2):
            j1 = j0 + 1
            home, s = j0 // 8, j0 % 8
            pair_lanes = (place == j0) | (place == j1)
            pair_rows = (sub == s) | (sub == s + 1)
            for b in range(batch):
                e, n = columns[b], rows[b]
                p, o, q = at(e[j0][home], s), at(e[j0][home], s + 1), at(e[j1][home], s + 1)
                r = reciprocal(p * q - o * o)
                w00, w01, w11 = q * r, -(o * r), p * r

                def mix(x0, x1):
                    return w00 * x0 + w01 * x1, w01 * x0 + w11 * x1

                m0, m1 = list(e[j0]), list(e[j1])
                m0[home] = jnp.where(sub == s, -1.0, jnp.where(sub == s + 1, 0.0, m0[home]))
                m1[home] = jnp.where(sub == s, 0.0, jnp.where(sub == s + 1, -1.0, m1[home]))
                for k in range(j1 + 1, panel):
                    f0, f1 = mix(at(e[k][home], s), at(e[k][home], s + 1))
                    for v in range(slabs):
                        base = jnp.where(pair_rows, 0.0, e[k][v]) if v == home else e[k][v]
                        e[k][v] = base - (m0[v] * f0 + m1[v] * f1)
                x0 = jnp.where(pair_lanes, jnp.where(place == j0, 1.0, 0.0), at(n[home], s))
                x1 = jnp.where(pair_lanes, jnp.where(place == j1, 1.0, 0.0), at(n[home], s + 1))
                r0, r1 = mix(x0, x1)
                for v in range(slabs):
                    gone = (pair_lanes | pair_rows) if v == home else pair_lanes
                    n[v] = jnp.where(gone, 0.0, n[v]) - (m0[v] * r0 + m1[v] * r1)
        lane_full = lax.broadcasted_iota(jnp.int32, (N, N), 1) - first
        row_full = lax.broadcasted_iota(jnp.int32, (N, N), 0) - first
        in_lanes = (lane_full >= 0) & (lane_full < panel)
        in_rows = (row_full >= 0) & (row_full < panel)
        for b in range(batch):
            old = work[b]
            work[b, pl.ds(first, panel), :] = jnp.concatenate(rows[b], axis=0)
            right = work[b]
            update = jnp.where(in_lanes, 0.0, old) - dot(jnp.where(in_lanes, old, 0.0), right)
            work[b] = jnp.where(in_rows, right, update)
        return carry

    lax.fori_loop(0, N // panel, step, 0)


def pad_rows(row):
    return jnp.broadcast_to(row, (8, N))


def solve_kernel(
    gram_ref, side_ref, kappa_ref, rate_ref, out_ref,
    work, keep, spread2, spread4, held, coupling, send, recv, send_x, recv_x, zs,
    send_sem, recv_sem, x_sems, *, chunks, owner,
):
    me = lax.axis_index("tm")
    chunk, tile = owner.chunk_of(me), owner.tile_of(me)
    levels = chunks.bit_length() - 1
    strides = [2 ** i for i in range(levels)]

    def device(other):
        return (owner.device(other, tile), lax.axis_index("obs"))

    stage_list = []
    for d in sorted(set([1] + strides)):
        stage_list += [-d, d]

    def exists(step):
        return jnp.logical_and(chunk + step >= 0, chunk + step < chunks)

    recv[...] = jnp.zeros_like(recv)
    recv_x[...] = jnp.zeros_like(recv_x)

    barrier = pltpu.get_barrier_semaphore()
    partners = 0
    for step in stage_list:
        @pl.when(exists(step))
        def _():
            pl.semaphore_signal(barrier, inc=1, device_id=device(chunk + step), device_id_type=MESH)
        partners = partners + exists(step).astype(jnp.int32)

    row_id = lax.broadcasted_iota(jnp.int32, (N, N), 0)
    lane_id = lax.broadcasted_iota(jnp.int32, (N, N), 1)
    end = jnp.logical_or(lane_id == 0, lane_id == N - 1)
    degree = jnp.where(end, 1.0, 2.0)
    prior = jnp.where(
        row_id == lane_id, kappa_ref[...] + degree,
        jnp.where(jnp.abs(row_id - lane_id) == 1, -1.0, 0.0),
    )
    weight_row = kappa_ref[...] + degree[:1]
    weight_column = jnp.sum(jnp.where(row_id == lane_id, prior, 0.0), axis=1, keepdims=True)

    def prior_left(m):
        up = jnp.where(row_id == 0, 0.0, pltpu.roll(m, 1, 0))
        down = jnp.where(row_id == N - 1, 0.0, pltpu.roll(m, N - 1, 0))
        return weight_column * m - up - down

    def prior_right(m):
        lanes = lax.broadcasted_iota(jnp.int32, m.shape, 1)
        up = jnp.where(lanes == 0, 0.0, pltpu.roll(m, 1, 1))
        down = jnp.where(lanes == N - 1, 0.0, pltpu.roll(m, N - 1, 1))
        return weight_row * m - up - down

    rates = [rate_ref[i] for i in range(SPAN + 1)]
    first = chunk == 0

    def diagonal(i):
        lead = 1.0
        if i == 0:
            lead = jnp.where(first, 1.0 - rates[0] * rates[0], 1.0)
        g = gram_ref[i]
        return (lead + rates[i + 1] * rates[i + 1]) * prior + 0.5 * (g + g.T)

    def side(i):
        return pad_rows(side_ref[i:i + 1, :])

    for b in range(4):
        work[b] = diagonal(2 * b + 1)
    invert(work, 4)
    sides = {i: side(i) for i in range(0, SPAN, 2)}
    after_side = jnp.zeros((8, N), F32)
    for b in range(4):
        i = 2 * b + 1
        inverse = work[b]
        keep[b] = inverse
        middle = prior_right(prior_left(inverse))
        z = dot(side(i), inverse)
        zs[i] = z
        pz = prior_right(z)
        low, high = rates[i], rates[i + 1]
        held[2 * b] = (diagonal(2 * b) if b == 0 else held[2 * b]) - (low * low) * middle
        coupling[b] = (-low * high) * middle
        sides[i - 1] = sides[i - 1] + low * pz
        if b < 3:
            held[2 * b + 2] = diagonal(2 * b + 2) - (high * high) * middle
            sides[i + 1] = sides[i + 1] + high * pz
        else:
            send[0, 0, 0:N, :] = (high * high) * middle
            after_side = after_side - high * pz

    work[0] = held[2]
    work[1] = held[6]
    invert(work, 2)
    for b, i in ((0, 2), (1, 6)):
        wide = jnp.concatenate([coupling[2 * b], coupling[2 * b + 1]], axis=1)
        tall = jnp.concatenate([coupling[2 * b], coupling[2 * b + 1]], axis=0)
        inverse = work[b]
        x = dot(inverse, wide)
        spread2[b] = x
        z = dot(sides[i], inverse)
        zs[i] = z
        vec = dot(z, wide)
        s = dot(tall, x)
        held[i - 2] = held[i - 2] - s[:N, :N]
        sides[i - 2] = sides[i - 2] - vec[:, :N]
        if b == 0:
            held[4] = held[4] - s[N:, N:]
            sides[4] = sides[4] - vec[:, N:]
            coupling[0] = -s[N:, :N]
            coupling[1] = -s[:N, N:]
        else:
            send[0, 0, 0:N, :] += s[N:, N:]
            after_side = after_side + vec[:, N:]
            coupling[2] = -s[:N, N:]
            coupling[3] = -s[N:, :N]

    work[0] = held[4]
    invert(work, 1)
    wide = jnp.concatenate([coupling[0], coupling[2]], axis=1)
    tall = jnp.concatenate([coupling[1], coupling[3]], axis=0)
    inverse = work[0]
    x = dot(inverse, wide)
    spread4[...] = x
    z = dot(sides[4], inverse)
    zs[4] = z
    vec = dot(z, wide)
    s = dot(tall, x)
    right = -s[:N, N:]
    send[0, 0, 0:N, :] += s[N:, N:]
    send[0, 0, N:2 * N, :] = s[N:, :N]
    send[0, 0, 2 * N:, :] = after_side + vec[:, N:]

    pl.semaphore_wait(barrier, partners)

    def copy(stage, way, step):
        return pltpu.make_async_remote_copy(
            src_ref=send.at[stage, way], dst_ref=recv.at[stage, way],
            send_sem=send_sem.at[stage, way], recv_sem=recv_sem.at[stage, way],
            device_id=device(chunk + step), device_id_type=MESH,
        )

    def start(stage, way, step):
        @pl.when(exists(step))
        def _():
            copy(stage, way, step).start()

    def arrive(stage, way, step):
        @pl.when(exists(-step))
        def _():
            copy(stage, way, step).wait_recv()

    start(0, 0, 1)
    diag = held[0] - s[:N, :N]
    vector = sides[0] - vec[:, :N]
    arrive(0, 0, 1)
    diag = diag - recv[0, 0, 0:N, :]
    left = -recv[0, 0, N:2 * N, :]
    vector = vector - recv[0, 0, 2 * N:, :]

    for stage, stride in enumerate(strides, 1):
        work[0] = diag
        invert(work, 1)
        inverse = work[0]
        wide = jnp.concatenate([left, right], axis=1)
        tall = jnp.concatenate([left.T, right.T], axis=0)
        x = dot(inverse, wide)
        z = dot(vector, inverse)
        vec = dot(z, wide)
        s = dot(tall, x)
        send[stage, 0, 0:N, :] = s[N:, N:]
        send[stage, 0, N:2 * N, :] = s[N:, :N]
        send[stage, 0, 2 * N:, :] = vec[:, N:]
        start(stage, 0, stride)
        send[stage, 1, 0:N, :] = s[:N, :N]
        send[stage, 1, N:2 * N, :] = s[:N, N:]
        send[stage, 1, 2 * N:, :] = vec[:, :N]
        start(stage, 1, -stride)
        arrive(stage, 0, stride)
        arrive(stage, 1, -stride)
        diag = diag - recv[stage, 0, 0:N, :] - recv[stage, 1, 0:N, :]
        left = -recv[stage, 0, N:2 * N, :]
        right = -recv[stage, 1, N:2 * N, :]
        vector = vector - recv[stage, 0, 2 * N:, :] - recv[stage, 1, 2 * N:, :]

    work[0] = diag
    invert(work, 1)
    x0 = dot(vector, work[0])
    send_x[...] = x0

    def copy_x():
        return pltpu.make_async_remote_copy(
            src_ref=send_x, dst_ref=recv_x, send_sem=x_sems.at[0], recv_sem=x_sems.at[1],
            device_id=device(chunk - 1), device_id_type=MESH,
        )

    @pl.when(exists(-1))
    def _():
        copy_x().start()

    @pl.when(exists(1))
    def _():
        copy_x().wait_recv()

    x8 = recv_x[...]
    found = {0: x0, 8: x8}
    last = ((1,), (1,))
    found[4] = zs[4] - dot(jnp.concatenate([x0, x8], axis=1), spread4[...], last)
    for b, i in ((0, 2), (1, 6)):
        found[i] = zs[i] - dot(jnp.concatenate([found[i - 2], found[i + 2]], axis=1), spread2[b], last)
    for b in range(4):
        i = 2 * b + 1
        mixed = rates[i] * found[i - 1] + rates[i + 1] * found[i + 1]
        found[i] = zs[i] + dot(prior_right(mixed), keep[b])
    out_ref[...] = jnp.concatenate([found[i][:1] for i in range(SPAN)], axis=0)

    @pl.when(exists(-1))
    def _():
        copy_x().wait_send()

    @pl.when(exists(1))
    def _():
        copy(0, 0, 1).wait_send()

    for stage, stride in enumerate(strides, 1):
        @pl.when(exists(stride))
        def _():
            copy(stage, 0, stride).wait_send()

        @pl.when(exists(-stride))
        def _():
            copy(stage, 1, -stride).wait_send()


class Consecutive:
    def chunk_of(self, me):
        return me // SPAN

    def tile_of(self, me):
        return me % SPAN

    def device(self, chunk, tile):
        return chunk * SPAN + tile


def solve(gram, side, kappa, rates, chunks):
    stages = chunks.bit_length()
    vmem = pl.BlockSpec(memory_space=pltpu.VMEM)
    return pl.pallas_call(
        functools.partial(solve_kernel, chunks=chunks, owner=Consecutive()),
        in_specs=[vmem, vmem, vmem, pl.BlockSpec(memory_space=pltpu.SMEM)],
        out_specs=vmem,
        out_shape=jax.ShapeDtypeStruct((SPAN, N), F32),
        scratch_shapes=[
            pltpu.VMEM((4, N, N), F32),
            pltpu.VMEM((4, N, N), F32),
            pltpu.VMEM((2, N, 2 * N), F32),
            pltpu.VMEM((N, 2 * N), F32),
            pltpu.VMEM((SPAN, N, N), F32),
            pltpu.VMEM((4, N, N), F32),
            pltpu.VMEM((stages, 2, 2 * N + 8, N), F32),
            pltpu.VMEM((stages, 2, 2 * N + 8, N), F32),
            pltpu.VMEM((8, N), F32),
            pltpu.VMEM((8, N), F32),
            pltpu.VMEM((SPAN, 8, N), F32),
            pltpu.SemaphoreType.DMA((stages, 2)),
            pltpu.SemaphoreType.DMA((stages, 2)),
            pltpu.SemaphoreType.DMA((2,)),
        ],
        compiler_params=pltpu.CompilerParams(
            collective_id=0, has_side_effects=True, vmem_limit_bytes=48 * 2**20
        ),
        name="solve",
    )(gram, side, kappa, rates)


def on_device(weights, tile_of, obs_prec, obs_value, node_kappa, rate):
    owned = node_kappa.shape[0] // N
    peers = lax.axis_size("obs")
    steps = lax.axis_size("tm")
    chunks = steps // SPAN
    me = lax.axis_index("tm")
    all_rates = lax.all_gather(rate[0], "tm")
    gram, side = tile_terms(weights[0], tile_of[0], obs_prec[0], obs_value[0], owned * peers)
    totals = lax.psum_scatter(
        jnp.concatenate([gram, side[:, None, :]], axis=1), "obs", scatter_dimension=0, tiled=True
    )
    groups = [[SPAN * c + k for k in range(SPAN)] for c in range(chunks)]
    mine = lax.all_to_all(totals, "tm", 0, 0, axis_index_groups=groups, tiled=True)
    chunk, tile = me // SPAN, me % SPAN
    kappa = lax.dynamic_slice(node_kappa.reshape(owned, N), (tile, 0), (1, N))
    padded = jnp.concatenate([all_rates, jnp.zeros((SPAN, owned), F32)], axis=0)
    rates = lax.dynamic_slice(padded, (chunk * SPAN, tile), (2 * SPAN, 1))[:, 0]
    states = solve(mine[:, :N], mine[:, N], kappa, rates, chunks)
    back = lax.all_to_all(states, "tm", 0, 0, axis_index_groups=groups, tiled=True)
    return back.reshape(1, owned * N)


def solution(mesh):
    placed = (
        P("tm", "obs", None),
        P("tm", "obs"),
        P("tm", "obs"),
        P("tm", "obs"),
        P("obs"),
        P("tm", "obs"),
    )
    return jax.shard_map(
        on_device, mesh=mesh, in_specs=placed, out_specs=P("tm", "obs"), check_vma=False
    )
```

```python
import functools

import jax
import jax.numpy as jnp
from jax import lax
from jax.experimental import pallas as pl
from jax.experimental.pallas import tpu as pltpu
from jax.sharding import PartitionSpec as P

F32 = jnp.float32
BF16 = jnp.bfloat16
N = 128
SPAN = 8
MESH = pl.DeviceIdType.MESH


def dot(left, right, dims=((1,), (0,))):
    return lax.dot_general(
        left, right, (dims, ((), ())), precision=lax.Precision.HIGHEST, preferred_element_type=F32
    )


class Owner:
    def chunk_of(self, me):
        return 2 * (me // 16) + me % 2

    def tile_of(self, me):
        return (me % 16) // 2

    def device(self, chunk, tile):
        return 16 * (chunk // 2) + 2 * tile + chunk % 2


OWNER = Owner()
FOLD = N // 2 + 8
DIAG, SIDE, RATE = N // 2, N // 2 + 1, N // 2 + 2


def fold(block, side):
    half = N // 2
    both = block + block.T
    row = lax.broadcasted_iota(jnp.int32, (half, N), 0)
    lane = lax.broadcasted_iota(jnp.int32, (half, N), 1) - half
    low = both[half:]
    packed = jnp.where((lane >= 0) & (lane <= row), pltpu.roll(both[:half], half, 1), low)
    diag = jnp.sum(jnp.where(lane == row, low, 0.0), axis=0, keepdims=True)
    sub = lax.broadcasted_iota(jnp.int32, (8, N), 0)
    extra = jnp.where(sub == 0, diag, jnp.where(sub == 1, side, 0.0))
    return jnp.concatenate([packed, extra], axis=0)


def unfold(packed):
    half = N // 2
    rows = packed[:half]
    turned = pltpu.roll(rows, half, 1)
    row = lax.broadcasted_iota(jnp.int32, (half, N), 0)
    lane = lax.broadcasted_iota(jnp.int32, (half, N), 1)
    top = jnp.where(lane < row, 0.5 * turned, jnp.where(lane == row, 0.25 * turned, 0.0))
    far = lane - half
    low = jnp.where(
        (far < 0) | (far > row), 0.5 * rows, jnp.where(far == row, 0.25 * packed[half:half + 1], 0.0)
    )
    both = jnp.concatenate([top, low], axis=0)
    return both + both.T


def front_kernel(
    rows_ref, label_ref, prec_ref, value_ref, rate_ref, out_ref, next_ref,
    scaled, paired, left, sides, send1, recv1, own, send2, recv2, send3, recv3,
    send1_sem, recv1_sem, send2_sem, recv2_sem, send3_sem, recv3_sem,
    *, chunks, peers,
):
    me, x = lax.axis_index("tm"), lax.axis_index("obs")
    plus, minus = lax.rem(x + 1, peers), lax.rem(x + peers - 1, peers)
    far = lax.rem(x + 2, peers)
    chunk, slot = me // SPAN, me % SPAN
    my_chunk, my_tile = OWNER.chunk_of(me), OWNER.tile_of(me)
    total_rows = rows_ref.shape[0]
    block = min(1024, total_rows)
    pairs = sides.shape[0]
    tell = jnp.logical_and(slot == 0, chunk > 0)
    told = my_chunk < chunks - 1

    barrier = pltpu.get_barrier_semaphore()
    awaited = 2
    for other in (plus, minus):
        pl.semaphore_signal(barrier, inc=1, device_id=(me, other), device_id_type=MESH)
    for i in range(SPAN):
        source = my_chunk * SPAN + i

        @pl.when(source != me)
        def _():
            pl.semaphore_signal(barrier, inc=1, device_id=(source, x), device_id_type=MESH)

        awaited = awaited + (OWNER.device(chunk, i) != me).astype(jnp.int32)
        awaited = awaited + jnp.logical_and(tell, OWNER.device(chunk - 1, i) != me).astype(jnp.int32)
    teller = (my_chunk + 1) * SPAN

    @pl.when(jnp.logical_and(told, teller != me))
    def _():
        pl.semaphore_signal(barrier, inc=1, device_id=(teller, x), device_id_type=MESH)

    pair = lax.shift_right_logical(label_ref[...], 1)
    odd = lax.bitwise_and(label_ref[...], 1)
    ones = lambda mask: jnp.where(mask, 1.0, 0.0).astype(BF16)
    for step in range(total_rows // block):
        here = slice(step * block, (step + 1) * block)
        turned = rows_ref[here, :].astype(F32).T
        scaled[:, here] = (turned * prec_ref[:, here]).astype(BF16)
        turned = turned.astype(BF16)
        paired[:N, here] = turned * ones(odd[:, here] == 0)
        paired[N:, here] = turned * ones(odd[:, here] == 1)
    last = (((1,), (1,)), ((), ()))
    part = prec_ref[...] * value_ref[...]
    match = lax.broadcasted_iota(jnp.int32, (pairs, total_rows), 0) == pair
    pieces = []
    for _ in range(3):
        top = part.astype(BF16).astype(F32)
        pieces.append(jnp.where(match, top, 0.0).astype(BF16))
        part = part - top
    side = lax.dot_general(
        jnp.concatenate(pieces, axis=0), paired[...], last, preferred_element_type=F32
    )
    sides[...] = side[:pairs] + side[pairs:2 * pairs] + side[2 * pairs:]

    def copy1(way, stage):
        return pltpu.make_async_remote_copy(
            src_ref=send1.at[way, stage], dst_ref=recv1.at[way, stage],
            send_sem=send1_sem.at[way, stage], recv_sem=recv1_sem.at[way, stage],
            device_id=(me, plus if way == 0 else minus), device_id_type=MESH,
        )

    def half(group, part, target, added=()):
        first = 4 * group + 2 * part
        for p in range(2):
            left[p * N:(p + 1) * N, :] = scaled[...] * ones(pair == first + p)
        total = lax.dot_general(left[...], paired[...], last, preferred_element_type=F32)
        for p in range(2):
            side_row = sides[pl.ds(first + p, 1), :]
            for o in range(2):
                q = 2 * p + o
                value = fold(
                    total[p * N:(p + 1) * N, o * N:(o + 1) * N], side_row[:, o * N:(o + 1) * N]
                )
                for way, stage in added:
                    value = value + recv1[way, stage, q]
                target[q] = value

    half(far, 0, send1.at[0, 0])
    half(far, 1, send1.at[1, 0])
    pl.semaphore_wait(barrier, awaited)
    copy1(0, 0).start()
    copy1(1, 0).start()

    def copy3(k):
        return pltpu.make_async_remote_copy(
            src_ref=send3.at[k], dst_ref=recv3, send_sem=send3_sem.at[k], recv_sem=recv3_sem.at[0],
            device_id=(OWNER.device(chunk - 1, k), x), device_id_type=MESH,
        )

    recv3_is_own = jnp.logical_and(told, teller == me)

    @pl.when(jnp.logical_not(told))
    def _():
        recv3[...] = jnp.zeros_like(recv3)

    @pl.when(tell)
    def _():
        for k in range(SPAN):
            send3[k] = full(rate_ref[:, k:k + 1])

            @pl.when(OWNER.device(chunk - 1, k) != me)
            def _():
                copy3(k).start()

    @pl.when(recv3_is_own)
    def _():
        recv3[...] = send3[my_tile]

    half(plus, 1, send1.at[0, 1])
    copy1(0, 1).start()
    half(minus, 0, send1.at[1, 1])
    copy1(1, 1).start()
    copy1(0, 0).wait_recv()
    half(plus, 0, send1.at[0, 2], [(0, 0)])
    copy1(0, 2).start()
    copy1(1, 0).wait_recv()
    half(minus, 1, send1.at[1, 2], [(1, 0)])
    copy1(1, 2).start()
    half(x, 0, own.at[0])
    half(x, 1, own.at[1])

    sub = lax.broadcasted_iota(jnp.int32, (8, N), 0)

    def copy2(k):
        return pltpu.make_async_remote_copy(
            src_ref=send2.at[k], dst_ref=recv2.at[slot],
            send_sem=send2_sem.at[k], recv_sem=recv2_sem.at[slot],
            device_id=(OWNER.device(chunk, k), x), device_id_type=MESH,
        )

    def arrival(i):
        return pltpu.make_async_remote_copy(
            src_ref=send2.at[0], dst_ref=recv2.at[i], send_sem=send2_sem.at[0], recv_sem=recv2_sem.at[i],
            device_id=(me, plus), device_id_type=MESH,
        )

    for part in range(2):
        copy1(part, 2).wait_recv()
        copy1(1 - part, 1).wait_recv()
        for q in range(4):
            k = 4 * part + q
            value = own[part, q] + recv1[part, 2, q] + recv1[1 - part, 1, q]
            send2[k, :N // 2] = value[:N // 2]
            send2[k, N // 2:] = jnp.where(sub == 2, full(rate_ref[:, k:k + 1]), value[N // 2:])
            mine = OWNER.device(chunk, k) == me

            @pl.when(jnp.logical_not(mine))
            def _():
                copy2(k).start()

            @pl.when(mine)
            def _():
                recv2[slot] = send2[k]

    for i in range(SPAN):
        @pl.when(my_chunk * SPAN + i != me)
        def _():
            arrival(i).wait_recv()

        out_ref[i] = recv2[i]

    @pl.when(jnp.logical_and(told, teller != me))
    def _():
        copy3(0).wait_recv()

    next_ref[...] = recv3[...]
    for way in range(2):
        for stage in range(3):
            copy1(way, stage).wait_send()
    for k in range(SPAN):
        @pl.when(OWNER.device(chunk, k) != me)
        def _():
            copy2(k).wait_send()

        @pl.when(jnp.logical_and(tell, OWNER.device(chunk - 1, k) != me))
        def _():
            copy3(k).wait_send()


def front(rows, label, prec, value, rate, chunks, peers):
    total_rows = rows.shape[0]
    row = lambda a: a.reshape(1, total_rows)
    vmem = pl.BlockSpec(memory_space=pltpu.VMEM)
    return pl.pallas_call(
        functools.partial(front_kernel, chunks=chunks, peers=peers),
        in_specs=[vmem] * 5,
        out_specs=[vmem, vmem],
        out_shape=[
            jax.ShapeDtypeStruct((SPAN, FOLD, N), F32),
            jax.ShapeDtypeStruct((8, N), F32),
        ],
        scratch_shapes=[
            pltpu.VMEM((N, total_rows), BF16),
            pltpu.VMEM((2 * N, total_rows), BF16),
            pltpu.VMEM((2 * N, total_rows), BF16),
            pltpu.VMEM((4 * peers, 2 * N), F32),
            pltpu.VMEM((2, 3, 4, FOLD, N), F32),
            pltpu.VMEM((2, 3, 4, FOLD, N), F32),
            pltpu.VMEM((2, 4, FOLD, N), F32),
            pltpu.VMEM((SPAN, FOLD, N), F32),
            pltpu.VMEM((SPAN, FOLD, N), F32),
            pltpu.VMEM((SPAN, 8, N), F32),
            pltpu.VMEM((8, N), F32),
            pltpu.SemaphoreType.DMA((2, 3)),
            pltpu.SemaphoreType.DMA((2, 3)),
            pltpu.SemaphoreType.DMA((SPAN,)),
            pltpu.SemaphoreType.DMA((SPAN,)),
            pltpu.SemaphoreType.DMA((SPAN,)),
            pltpu.SemaphoreType.DMA((1,)),
        ],
        compiler_params=pltpu.CompilerParams(
            collective_id=1, has_side_effects=True, vmem_limit_bytes=48 * 2**20
        ),
        name="front",
    )(rows, row(label), row(prec), row(value), rate)


def reciprocal(x):
    r = pltpu.reciprocal(x, approx=True)
    r = r * (2.0 - x * r)
    return r * (2.0 - x * r)
def full(x):
    return jnp.broadcast_to(x, (8, N))
def invert(work, batch):
    panel = 16
    slabs = panel // 8
    lane = lax.broadcasted_iota(jnp.int32, (8, N), 1)
    sub = lax.broadcasted_iota(jnp.int32, (8, N), 0)
    at = lambda x, s: full(x[s:s + 1, :])

    def load(first, b):
        return [work[b, pl.ds(pl.multiple_of(first + 8 * v, 8), 8), :] for v in range(slabs)]

    def spread(mats, first):
        picks = [jnp.full((8, N), k, jnp.int32) + first for k in range(panel)]
        return [
            [jnp.take_along_axis(m, pick, axis=1, mode="promise_in_bounds") for m in mats] for pick in picks
        ]

    def step(index, carry):
        first = pl.multiple_of(index * panel, panel)
        rows = [load(first, b) for b in range(batch)]
        columns = [spread(rows[b], first) for b in range(batch)]
        place = lane - first
        for j0 in range(0, panel, 2):
            j1 = j0 + 1
            home, s = j0 // 8, j0 % 8
            pair_lanes = (place == j0) | (place == j1)
            pair_rows = (sub == s) | (sub == s + 1)
            for b in range(batch):
                e, n = columns[b], rows[b]
                p, o, q = at(e[j0][home], s), at(e[j0][home], s + 1), at(e[j1][home], s + 1)
                r = reciprocal(p * q - o * o)
                w00, w01, w11 = q * r, -(o * r), p * r

                def mix(x0, x1):
                    return w00 * x0 + w01 * x1, w01 * x0 + w11 * x1

                m0, m1 = list(e[j0]), list(e[j1])
                m0[home] = jnp.where(sub == s, -1.0, jnp.where(sub == s + 1, 0.0, m0[home]))
                m1[home] = jnp.where(sub == s, 0.0, jnp.where(sub == s + 1, -1.0, m1[home]))
                for k in range(j1 + 1, panel):
                    f0, f1 = mix(at(e[k][home], s), at(e[k][home], s + 1))
                    for v in range(slabs):
                        base = jnp.where(pair_rows, 0.0, e[k][v]) if v == home else e[k][v]
                        e[k][v] = base - (m0[v] * f0 + m1[v] * f1)
                x0 = jnp.where(pair_lanes, jnp.where(place == j0, 1.0, 0.0), at(n[home], s))
                x1 = jnp.where(pair_lanes, jnp.where(place == j1, 1.0, 0.0), at(n[home], s + 1))
                r0, r1 = mix(x0, x1)
                for v in range(slabs):
                    gone = (pair_lanes | pair_rows) if v == home else pair_lanes
                    n[v] = jnp.where(gone, 0.0, n[v]) - (m0[v] * r0 + m1[v] * r1)
        lane_full = lax.broadcasted_iota(jnp.int32, (N, N), 1) - first
        row_full = lax.broadcasted_iota(jnp.int32, (N, N), 0) - first
        in_lanes = (lane_full >= 0) & (lane_full < panel)
        in_rows = (row_full >= 0) & (row_full < panel)
        for b in range(batch):
            old = work[b]
            work[b, pl.ds(first, panel), :] = jnp.concatenate(rows[b], axis=0)
            right = work[b]
            update = jnp.where(in_lanes, 0.0, old) - dot(jnp.where(in_lanes, old, 0.0), right)
            work[b] = jnp.where(in_rows, right, update)
        return carry

    lax.fori_loop(0, N // panel, step, 0)


def pad_rows(row):
    return jnp.broadcast_to(row, (8, N))


def solve_kernel(
    packed_ref, next_ref, kappa_ref, out_ref,
    work, keep, spread2, spread4, held, coupling, send, recv, send_x, recv_x, zs, send_out, recv_out,
    send_sem, recv_sem, x_sems, send_out_sem, recv_out_sem, *, chunks,
):
    me = lax.axis_index("tm")
    chunk, tile = OWNER.chunk_of(me), OWNER.tile_of(me)
    home, place = me // SPAN, me % SPAN
    levels = chunks.bit_length() - 1
    strides = [2 ** i for i in range(levels)]

    def device(other):
        return (OWNER.device(other, tile), lax.axis_index("obs"))

    stage_list = []
    for d in sorted(set([1] + strides)):
        stage_list += [-d, d]

    def exists(step):
        return jnp.logical_and(chunk + step >= 0, chunk + step < chunks)

    recv[...] = jnp.zeros_like(recv)
    recv_x[...] = jnp.zeros_like(recv_x)

    barrier = pltpu.get_barrier_semaphore()
    partners = 0
    for step in stage_list:
        @pl.when(exists(step))
        def _():
            pl.semaphore_signal(barrier, inc=1, device_id=device(chunk + step), device_id_type=MESH)
        partners = partners + exists(step).astype(jnp.int32)
    for i in range(SPAN):
        @pl.when(OWNER.device(home, i) != me)
        def _():
            pl.semaphore_signal(
                barrier, inc=1, device_id=(OWNER.device(home, i), lax.axis_index("obs")), device_id_type=MESH
            )
        partners = partners + (chunk * SPAN + i != me).astype(jnp.int32)

    row_id = lax.broadcasted_iota(jnp.int32, (N, N), 0)
    lane_id = lax.broadcasted_iota(jnp.int32, (N, N), 1)
    end = jnp.logical_or(lane_id == 0, lane_id == N - 1)
    degree = jnp.where(end, 1.0, 2.0)
    prior = jnp.where(
        row_id == lane_id, kappa_ref[...] + degree,
        jnp.where(jnp.abs(row_id - lane_id) == 1, -1.0, 0.0),
    )
    weight_row = kappa_ref[...] + degree[:1]
    weight_column = jnp.sum(jnp.where(row_id == lane_id, prior, 0.0), axis=1, keepdims=True)

    def prior_left(m):
        up = jnp.where(row_id == 0, 0.0, pltpu.roll(m, 1, 0))
        down = jnp.where(row_id == N - 1, 0.0, pltpu.roll(m, N - 1, 0))
        return weight_column * m - up - down

    def prior_right(m):
        lanes = lax.broadcasted_iota(jnp.int32, m.shape, 1)
        up = jnp.where(lanes == 0, 0.0, pltpu.roll(m, 1, 1))
        down = jnp.where(lanes == N - 1, 0.0, pltpu.roll(m, N - 1, 1))
        return weight_row * m - up - down

    rates = [packed_ref[i, RATE:RATE + 1, :] for i in range(SPAN)] + [next_ref[:1]]
    first = chunk == 0

    def diagonal(i):
        lead = 1.0
        if i == 0:
            lead = jnp.where(first, 1.0 - rates[0] * rates[0], 1.0)
        return (lead + rates[i + 1] * rates[i + 1]) * prior + unfold(packed_ref[i])

    def side(i):
        return pad_rows(packed_ref[i, SIDE:SIDE + 1, :])

    for b in range(4):
        work[b] = diagonal(2 * b + 1)
    invert(work, 4)
    sides = {i: side(i) for i in range(0, SPAN, 2)}
    after_side = jnp.zeros((8, N), F32)
    for b in range(4):
        i = 2 * b + 1
        inverse = work[b]
        keep[b] = inverse
        middle = prior_right(prior_left(inverse))
        z = dot(side(i), inverse)
        zs[i] = z
        pz = prior_right(z)
        low, high = rates[i], rates[i + 1]
        held[2 * b] = (diagonal(2 * b) if b == 0 else held[2 * b]) - (low * low) * middle
        coupling[b] = (-low * high) * middle
        sides[i - 1] = sides[i - 1] + low * pz
        if b < 3:
            held[2 * b + 2] = diagonal(2 * b + 2) - (high * high) * middle
            sides[i + 1] = sides[i + 1] + high * pz
        else:
            send[0, 0, 0:N, :] = (high * high) * middle
            after_side = after_side - high * pz

    work[0] = held[2]
    work[1] = held[6]
    invert(work, 2)
    for b, i in ((0, 2), (1, 6)):
        wide = jnp.concatenate([coupling[2 * b], coupling[2 * b + 1]], axis=1)
        tall = jnp.concatenate([coupling[2 * b], coupling[2 * b + 1]], axis=0)
        inverse = work[b]
        x = dot(inverse, wide)
        spread2[b] = x
        z = dot(sides[i], inverse)
        zs[i] = z
        vec = dot(z, wide)
        s = dot(tall, x)
        held[i - 2] = held[i - 2] - s[:N, :N]
        sides[i - 2] = sides[i - 2] - vec[:, :N]
        if b == 0:
            held[4] = held[4] - s[N:, N:]
            sides[4] = sides[4] - vec[:, N:]
            coupling[0] = -s[N:, :N]
            coupling[1] = -s[:N, N:]
        else:
            send[0, 0, 0:N, :] += s[N:, N:]
            after_side = after_side + vec[:, N:]
            coupling[2] = -s[:N, N:]
            coupling[3] = -s[N:, :N]

    work[0] = held[4]
    invert(work, 1)
    wide = jnp.concatenate([coupling[0], coupling[2]], axis=1)
    tall = jnp.concatenate([coupling[1], coupling[3]], axis=0)
    inverse = work[0]
    x = dot(inverse, wide)
    spread4[...] = x
    z = dot(sides[4], inverse)
    zs[4] = z
    vec = dot(z, wide)
    s = dot(tall, x)
    right = -s[:N, N:]
    send[0, 0, 0:N, :] += s[N:, N:]
    send[0, 0, N:2 * N, :] = s[N:, :N]
    send[0, 0, 2 * N:, :] = after_side + vec[:, N:]

    pl.semaphore_wait(barrier, partners)

    def copy(stage, way, step):
        return pltpu.make_async_remote_copy(
            src_ref=send.at[stage, way], dst_ref=recv.at[stage, way],
            send_sem=send_sem.at[stage, way], recv_sem=recv_sem.at[stage, way],
            device_id=device(chunk + step), device_id_type=MESH,
        )

    def start(stage, way, step):
        @pl.when(exists(step))
        def _():
            copy(stage, way, step).start()

    def arrive(stage, way, step):
        @pl.when(exists(-step))
        def _():
            copy(stage, way, step).wait_recv()

    start(0, 0, 1)
    diag = held[0] - s[:N, :N]
    vector = sides[0] - vec[:, :N]
    arrive(0, 0, 1)
    diag = diag - recv[0, 0, 0:N, :]
    left = -recv[0, 0, N:2 * N, :]
    vector = vector - recv[0, 0, 2 * N:, :]

    for stage, stride in enumerate(strides, 1):
        work[0] = diag
        invert(work, 1)
        inverse = work[0]
        wide = jnp.concatenate([left, right], axis=1)
        tall = jnp.concatenate([left.T, right.T], axis=0)
        x = dot(inverse, wide)
        z = dot(vector, inverse)
        vec = dot(z, wide)
        s = dot(tall, x)
        send[stage, 0, 0:N, :] = s[N:, N:]
        send[stage, 0, N:2 * N, :] = s[N:, :N]
        send[stage, 0, 2 * N:, :] = vec[:, N:]
        start(stage, 0, stride)
        send[stage, 1, 0:N, :] = s[:N, :N]
        send[stage, 1, N:2 * N, :] = s[:N, N:]
        send[stage, 1, 2 * N:, :] = vec[:, :N]
        start(stage, 1, -stride)
        arrive(stage, 0, stride)
        arrive(stage, 1, -stride)
        diag = diag - recv[stage, 0, 0:N, :] - recv[stage, 1, 0:N, :]
        left = -recv[stage, 0, N:2 * N, :]
        right = -recv[stage, 1, N:2 * N, :]
        vector = vector - recv[stage, 0, 2 * N:, :] - recv[stage, 1, 2 * N:, :]

    work[0] = diag
    invert(work, 1)
    x0 = dot(vector, work[0])
    send_x[...] = x0

    def copy_x():
        return pltpu.make_async_remote_copy(
            src_ref=send_x, dst_ref=recv_x, send_sem=x_sems.at[0], recv_sem=x_sems.at[1],
            device_id=device(chunk - 1), device_id_type=MESH,
        )

    @pl.when(exists(-1))
    def _():
        copy_x().start()

    @pl.when(exists(1))
    def _():
        copy_x().wait_recv()

    x8 = recv_x[...]
    found = {0: x0, 8: x8}
    last = ((1,), (1,))
    found[4] = zs[4] - dot(jnp.concatenate([x0, x8], axis=1), spread4[...], last)
    for b, i in ((0, 2), (1, 6)):
        found[i] = zs[i] - dot(jnp.concatenate([found[i - 2], found[i + 2]], axis=1), spread2[b], last)
    for b in range(4):
        i = 2 * b + 1
        mixed = rates[i] * found[i - 1] + rates[i + 1] * found[i + 1]
        found[i] = zs[i] + dot(prior_right(mixed), keep[b])
    def copy_out(i):
        return pltpu.make_async_remote_copy(
            src_ref=send_out.at[i], dst_ref=recv_out.at[tile],
            send_sem=send_out_sem.at[i], recv_sem=recv_out_sem.at[tile],
            device_id=(chunk * SPAN + i, lax.axis_index("obs")), device_id_type=MESH,
        )

    def arrive_out(k):
        return pltpu.make_async_remote_copy(
            src_ref=send_out.at[0], dst_ref=recv_out.at[k],
            send_sem=send_out_sem.at[0], recv_sem=recv_out_sem.at[k],
            device_id=(OWNER.device(home, k), lax.axis_index("obs")), device_id_type=MESH,
        )

    for i in range(SPAN):
        send_out[i] = found[i]

        @pl.when(chunk * SPAN + i != me)
        def _():
            copy_out(i).start()

        @pl.when(chunk * SPAN + i == me)
        def _():
            recv_out[tile] = send_out[i]

    for k in range(SPAN):
        @pl.when(OWNER.device(home, k) != me)
        def _():
            arrive_out(k).wait_recv()

        out_ref[:, k * N:(k + 1) * N] = recv_out[k, :1, :]

    for i in range(SPAN):
        @pl.when(chunk * SPAN + i != me)
        def _():
            copy_out(i).wait_send()

    @pl.when(exists(-1))
    def _():
        copy_x().wait_send()

    @pl.when(exists(1))
    def _():
        copy(0, 0, 1).wait_send()

    for stage, stride in enumerate(strides, 1):
        @pl.when(exists(stride))
        def _():
            copy(stage, 0, stride).wait_send()

        @pl.when(exists(-stride))
        def _():
            copy(stage, 1, -stride).wait_send()


def solve(packed, after, kappa, chunks):
    stages = chunks.bit_length()
    vmem = pl.BlockSpec(memory_space=pltpu.VMEM)
    return pl.pallas_call(
        functools.partial(solve_kernel, chunks=chunks),
        in_specs=[vmem] * 3,
        out_specs=vmem,
        out_shape=jax.ShapeDtypeStruct((1, SPAN * N), F32),
        scratch_shapes=[
            pltpu.VMEM((4, N, N), F32),
            pltpu.VMEM((4, N, N), F32),
            pltpu.VMEM((2, N, 2 * N), F32),
            pltpu.VMEM((N, 2 * N), F32),
            pltpu.VMEM((SPAN, N, N), F32),
            pltpu.VMEM((4, N, N), F32),
            pltpu.VMEM((stages, 2, 2 * N + 8, N), F32),
            pltpu.VMEM((stages, 2, 2 * N + 8, N), F32),
            pltpu.VMEM((8, N), F32),
            pltpu.VMEM((8, N), F32),
            pltpu.VMEM((SPAN, 8, N), F32),
            pltpu.VMEM((SPAN, 8, N), F32),
            pltpu.VMEM((SPAN, 8, N), F32),
            pltpu.SemaphoreType.DMA((stages, 2)),
            pltpu.SemaphoreType.DMA((stages, 2)),
            pltpu.SemaphoreType.DMA((2,)),
            pltpu.SemaphoreType.DMA((SPAN,)),
            pltpu.SemaphoreType.DMA((SPAN,)),
        ],
        compiler_params=pltpu.CompilerParams(
            collective_id=0, has_side_effects=True, vmem_limit_bytes=48 * 2**20
        ),
        name="solve",
    )(packed, after, kappa)


def on_device(weights, tile_of, obs_prec, obs_value, node_kappa, rate):
    owned = node_kappa.shape[0] // N
    chunks = lax.axis_size("tm") // SPAN
    tile = OWNER.tile_of(lax.axis_index("tm"))
    packed, after = front(
        weights[0], tile_of[0], obs_prec[0], obs_value[0], rate, chunks, lax.axis_size("obs")
    )
    kappa = lax.dynamic_slice(node_kappa.reshape(owned, N), (tile, 0), (1, N))
    return solve(packed, after, kappa, chunks)


def solution(mesh):
    placed = (
        P("tm", "obs", None),
        P("tm", "obs"),
        P("tm", "obs"),
        P("tm", "obs"),
        P("obs"),
        P("tm", "obs"),
    )
    return jax.shard_map(
        on_device, mesh=mesh, in_specs=placed, out_specs=P("tm", "obs"), check_vma=False
    )
```

```python
import functools

import jax
import jax.numpy as jnp
from jax import lax
from jax.experimental import pallas as pl
from jax.experimental.pallas import tpu as pltpu
from jax.sharding import PartitionSpec as P

F32 = jnp.float32
BF16 = jnp.bfloat16
N = 128
SPAN = 8
MESH = pl.DeviceIdType.MESH


def dot(left, right, dims=((1,), (0,))):
    return lax.dot_general(
        left, right, (dims, ((), ())), precision=lax.Precision.HIGHEST, preferred_element_type=F32
    )


class Owner:
    def chunk_of(self, me):
        return 2 * (me // 16) + me % 2

    def tile_of(self, me):
        return (me % 16) // 2

    def device(self, chunk, tile):
        return 16 * (chunk // 2) + 2 * tile + chunk % 2


OWNER = Owner()
FOLD = N // 2 + 8
DIAG, SIDE, RATE = N // 2, N // 2 + 1, N // 2 + 2


def fold(block, side):
    half = N // 2
    both = block + block.T
    row = lax.broadcasted_iota(jnp.int32, (half, N), 0)
    lane = lax.broadcasted_iota(jnp.int32, (half, N), 1) - half
    low = both[half:]
    packed = jnp.where((lane >= 0) & (lane <= row), pltpu.roll(both[:half], half, 1), low)
    diag = jnp.sum(jnp.where(lane == row, low, 0.0), axis=0, keepdims=True)
    sub = lax.broadcasted_iota(jnp.int32, (8, N), 0)
    extra = jnp.where(sub == 0, diag, jnp.where(sub == 1, side, 0.0))
    return jnp.concatenate([packed, extra], axis=0)


def unfold(packed):
    half = N // 2
    rows = packed[:half]
    turned = pltpu.roll(rows, half, 1)
    row = lax.broadcasted_iota(jnp.int32, (half, N), 0)
    lane = lax.broadcasted_iota(jnp.int32, (half, N), 1)
    top = jnp.where(lane < row, 0.5 * turned, jnp.where(lane == row, 0.25 * turned, 0.0))
    far = lane - half
    low = jnp.where(
        (far < 0) | (far > row), 0.5 * rows, jnp.where(far == row, 0.25 * packed[half:half + 1], 0.0)
    )
    both = jnp.concatenate([top, low], axis=0)
    return both + both.T


def front_part(
    rows_hbm, label_hbm, prec_hbm, value_hbm, rate_hbm, kappa_hbm,
    rows_ref, label_ref, prec_ref, value_ref, rate_ref, kappa_ref,
    scaled, paired, left, sides, send1, recv1, own, send2, recv2, send3, recv3,
    load_sem, send1_sem, recv1_sem, send2_sem, recv2_sem, send3_sem, recv3_sem,
    *, chunks, peers,
):
    me, x = lax.axis_index("tm"), lax.axis_index("obs")
    plus, minus = lax.rem(x + 1, peers), lax.rem(x + peers - 1, peers)
    far = lax.rem(x + 2, peers)
    chunk, slot = me // SPAN, me % SPAN
    my_chunk, my_tile = OWNER.chunk_of(me), OWNER.tile_of(me)
    total_rows = rows_ref.shape[0]
    block = min(1024, total_rows)
    pairs = sides.shape[0]
    loads = [
        pltpu.make_async_copy(source, target, load_sem.at[i])
        for i, (source, target) in enumerate(
            (
                (label_hbm, label_ref), (prec_hbm, prec_ref), (value_hbm, value_ref),
                (rate_hbm, rate_ref), (kappa_hbm, kappa_ref),
            )
        )
    ]
    row_loads = [
        pltpu.make_async_copy(
            rows_hbm.at[0, pl.ds(i * block, block)], rows_ref.at[pl.ds(i * block, block)], load_sem.at[len(loads) + i]
        )
        for i in range(total_rows // block)
    ]
    for load in loads + row_loads:
        load.start()
    tell = jnp.logical_and(slot == 0, chunk > 0)
    told = my_chunk < chunks - 1

    barrier = pltpu.get_barrier_semaphore()
    awaited = 2
    for other in (plus, minus):
        pl.semaphore_signal(barrier, inc=1, device_id=(me, other), device_id_type=MESH)
    for i in range(SPAN):
        source = my_chunk * SPAN + i

        @pl.when(source != me)
        def _():
            pl.semaphore_signal(barrier, inc=1, device_id=(source, x), device_id_type=MESH)

        awaited = awaited + (OWNER.device(chunk, i) != me).astype(jnp.int32)
        awaited = awaited + jnp.logical_and(tell, OWNER.device(chunk - 1, i) != me).astype(jnp.int32)
    teller = (my_chunk + 1) * SPAN

    @pl.when(jnp.logical_and(told, teller != me))
    def _():
        pl.semaphore_signal(barrier, inc=1, device_id=(teller, x), device_id_type=MESH)

    for stride in [2 ** i for i in range(max(1, chunks.bit_length() - 1))]:
        for other in (my_chunk - stride, my_chunk + stride):
            exists = jnp.logical_and(other >= 0, other < chunks)

            @pl.when(exists)
            def _():
                pl.semaphore_signal(
                    barrier, inc=1, device_id=(OWNER.device(other, my_tile), x), device_id_type=MESH
                )

            awaited = awaited + exists.astype(jnp.int32)
    for i in range(SPAN):
        source = OWNER.device(chunk, i)

        @pl.when(source != me)
        def _():
            pl.semaphore_signal(barrier, inc=1, device_id=(source, x), device_id_type=MESH)

        awaited = awaited + (my_chunk * SPAN + i != me).astype(jnp.int32)

    for load in loads:
        load.wait()
    pair = lax.shift_right_logical(label_ref[...], 1)
    odd = lax.bitwise_and(label_ref[...], 1)
    ones = lambda mask: jnp.where(mask, 1.0, 0.0).astype(BF16)
    for step in range(total_rows // block):
        here = slice(step * block, (step + 1) * block)
        row_loads[step].wait()
        turned = rows_ref[here, :].astype(F32).T
        scaled[:, here] = (turned * prec_ref[:, here]).astype(BF16)
        turned = turned.astype(BF16)
        paired[:N, here] = turned * ones(odd[:, here] == 0)
        paired[N:, here] = turned * ones(odd[:, here] == 1)
    last = (((1,), (1,)), ((), ()))
    part = prec_ref[...] * value_ref[...]
    match = lax.broadcasted_iota(jnp.int32, (pairs, total_rows), 0) == pair
    pieces = []
    for _ in range(3):
        top = part.astype(BF16).astype(F32)
        pieces.append(jnp.where(match, top, 0.0).astype(BF16))
        part = part - top
    side = lax.dot_general(
        jnp.concatenate(pieces, axis=0), paired[...], last, preferred_element_type=F32
    )
    sides[...] = side[:pairs] + side[pairs:2 * pairs] + side[2 * pairs:]

    def copy1(way, stage, q=None):
        piece = (way, stage) if q is None else (way, stage, q)
        sem = stage + (q or 0)
        return pltpu.make_async_remote_copy(
            src_ref=send1.at[piece], dst_ref=recv1.at[piece],
            send_sem=send1_sem.at[way, sem], recv_sem=recv1_sem.at[way, sem],
            device_id=(me, plus if way == 0 else minus), device_id_type=MESH,
        )

    def half(group, part, target, added=()):
        first = 4 * group + 2 * part
        for p in range(2):
            left[p * N:(p + 1) * N, :] = scaled[...] * ones(pair == first + p)
        total = lax.dot_general(left[...], paired[...], last, preferred_element_type=F32)
        for p in range(2):
            side_row = sides[pl.ds(first + p, 1), :]
            for o in range(2):
                q = 2 * p + o
                value = fold(
                    total[p * N:(p + 1) * N, o * N:(o + 1) * N], side_row[:, o * N:(o + 1) * N]
                )
                for way, stage in added:
                    value = value + recv1[way, stage, q]
                target[q] = value

    half(far, 0, send1.at[0, 0])
    half(far, 1, send1.at[1, 0])
    pl.semaphore_wait(barrier, awaited)
    copy1(0, 0).start()
    copy1(1, 0).start()

    def copy3(k):
        return pltpu.make_async_remote_copy(
            src_ref=send3.at[k], dst_ref=recv3, send_sem=send3_sem.at[k], recv_sem=recv3_sem.at[0],
            device_id=(OWNER.device(chunk - 1, k), x), device_id_type=MESH,
        )

    recv3_is_own = jnp.logical_and(told, teller == me)

    @pl.when(jnp.logical_not(told))
    def _():
        recv3[...] = jnp.zeros_like(recv3)

    @pl.when(tell)
    def _():
        for k in range(SPAN):
            send3[k] = full(rate_ref[:, k:k + 1])

            @pl.when(OWNER.device(chunk - 1, k) != me)
            def _():
                copy3(k).start()

    @pl.when(recv3_is_own)
    def _():
        recv3[...] = send3[my_tile]

    half(plus, 1, send1.at[0, 1])
    copy1(0, 1).start()
    half(minus, 0, send1.at[1, 1])
    copy1(1, 1).start()
    copy1(0, 0).wait_recv()
    half(plus, 0, send1.at[0, 2], [(0, 0)])
    for q in range(4):
        copy1(0, 2, q).start()
    copy1(1, 0).wait_recv()
    half(minus, 1, send1.at[1, 2], [(1, 0)])
    for q in range(4):
        copy1(1, 2, q).start()
    half(x, 0, own.at[0])
    half(x, 1, own.at[1])

    sub = lax.broadcasted_iota(jnp.int32, (8, N), 0)

    def copy2(k):
        return pltpu.make_async_remote_copy(
            src_ref=send2.at[k], dst_ref=recv2.at[slot],
            send_sem=send2_sem.at[k], recv_sem=recv2_sem.at[slot],
            device_id=(OWNER.device(chunk, k), x), device_id_type=MESH,
        )

    def arrival(i):
        return pltpu.make_async_remote_copy(
            src_ref=send2.at[0], dst_ref=recv2.at[i], send_sem=send2_sem.at[0], recv_sem=recv2_sem.at[i],
            device_id=(me, plus), device_id_type=MESH,
        )

    copy1(0, 1).wait_recv()
    copy1(1, 1).wait_recv()
    for q in range(4):
        for part in range(2):
            copy1(part, 2, q).wait_recv()
            k = 4 * part + q
            value = own[part, q] + recv1[part, 2, q] + recv1[1 - part, 1, q]
            send2[k, :N // 2] = value[:N // 2]
            send2[k, N // 2:] = jnp.where(sub == 2, full(rate_ref[:, k:k + 1]), value[N // 2:])
            mine = OWNER.device(chunk, k) == me

            @pl.when(jnp.logical_not(mine))
            def _():
                copy2(k).start()

            @pl.when(mine)
            def _():
                recv2[slot] = send2[k]

    for i in range(SPAN):
        @pl.when(my_chunk * SPAN + i != me)
        def _():
            arrival(i).wait_recv()

    @pl.when(jnp.logical_and(told, teller != me))
    def _():
        copy3(0).wait_recv()

    def finish():
        for way in range(2):
            copy1(way, 0).wait_send()
            copy1(way, 1).wait_send()
            for q in range(4):
                copy1(way, 2, q).wait_send()
        for k in range(SPAN):
            @pl.when(OWNER.device(chunk, k) != me)
            def _():
                copy2(k).wait_send()

            @pl.when(jnp.logical_and(tell, OWNER.device(chunk - 1, k) != me))
            def _():
                copy3(k).wait_send()

    return finish


def reciprocal(x):
    r = pltpu.reciprocal(x, approx=True)
    r = r * (2.0 - x * r)
    return r * (2.0 - x * r)

def full(x):
    return jnp.broadcast_to(x, (8, N))

def tree_sum(parts):
    while len(parts) > 1:
        parts = [parts[x] + parts[x + 1] for x in range(0, len(parts), 2)]
    return parts[0]


def invert(work, batch, panel=16):
    unroll = 2 if batch <= 2 else 1
    slabs = panel // 8
    lane = lax.broadcasted_iota(jnp.int32, (8, N), 1)
    sub = lax.broadcasted_iota(jnp.int32, (8, N), 0)
    lane_full = lax.broadcasted_iota(jnp.int32, (N, N), 1)
    row_full = lax.broadcasted_iota(jnp.int32, (N, N), 0)
    at = lambda x, s: full(x[s:s + 1, :])

    def load(first, b):
        return [work[b, pl.ds(pl.multiple_of(first + 8 * v, 8), 8), :] for v in range(slabs)]

    def spread(mats, first):
        picks = [jnp.full((8, N), k, jnp.int32) + first for k in range(panel)]
        return [[jnp.take_along_axis(m, pick, axis=1, mode="promise_in_bounds") for m in mats] for pick in picks]

    def update(first, b):
        in_lanes = (lane_full >= first) & (lane_full < first + panel)
        in_rows = (row_full >= first) & (row_full < first + panel)
        old = work[b]
        change = dot(jnp.where(in_lanes & ~in_rows, old, 0.0), old)
        return jnp.where(in_lanes & ~in_rows, 0.0, old) - change

    def step(index, carry):
        first = pl.multiple_of(index * panel, panel)
        after = pl.multiple_of(lax.rem(first + panel, N), panel)
        rows = [[carry[b * slabs + v] for v in range(slabs)] for b in range(batch)]
        columns = [spread(rows[b], first) for b in range(batch)]
        place = lane - first
        inside = (place >= 0) & (place < panel)
        for b in range(batch):
            work[b] = update(first - panel, b)
        coming = [load(after, b) for b in range(batch)]
        below = [spread(coming[b], first) for b in range(batch)]
        for j0 in range(0, panel, 2):
            j1 = j0 + 1
            home, s = j0 // 8, j0 % 8
            pair_lanes = (place == j0) | (place == j1)
            pair_rows = (sub == s) | (sub == s + 1)
            for b in range(batch):
                e, n = columns[b], rows[b]
                p, o, q = at(e[j0][home], s), at(e[j0][home], s + 1), at(e[j1][home], s + 1)
                r = reciprocal(p * q - o * o)
                w00, w01, w11 = q * r, -(o * r), p * r

                def mix(x0, x1):
                    return w00 * x0 + w01 * x1, w01 * x0 + w11 * x1

                m0, m1 = list(e[j0]), list(e[j1])
                m0[home] = jnp.where(sub == s, -1.0, jnp.where(sub == s + 1, 0.0, m0[home]))
                m1[home] = jnp.where(sub == s, 0.0, jnp.where(sub == s + 1, -1.0, m1[home]))
                for k in range(j1 + 1, panel):
                    f0, f1 = mix(at(e[k][home], s), at(e[k][home], s + 1))
                    for v in range(slabs):
                        base = jnp.where(pair_rows, 0.0, e[k][v]) if v == home else e[k][v]
                        e[k][v] = base - (m0[v] * f0 + m1[v] * f1)
                x0 = jnp.where(pair_lanes, jnp.where(place == j0, 1.0, 0.0), at(n[home], s))
                x1 = jnp.where(pair_lanes, jnp.where(place == j1, 1.0, 0.0), at(n[home], s + 1))
                r0, r1 = mix(x0, x1)
                for v in range(slabs):
                    gone = (pair_lanes | pair_rows) if v == home else pair_lanes
                    n[v] = jnp.where(gone, 0.0, n[v]) - (m0[v] * r0 + m1[v] * r1)
        out = []
        for b in range(batch):
            work[b, pl.ds(first, panel), :] = jnp.concatenate(rows[b], axis=0)
            out += [
                jnp.where(inside, 0.0, coming[b][v])
                - tree_sum([below[b][k][v] * at(rows[b][k // 8], k % 8) for k in range(panel)])
                for v in range(slabs)
            ]
        return tuple(out)

    def steps(index, carry):
        for i in range(unroll):
            carry = step(index * unroll + i, carry)
        return carry
    lax.fori_loop(0, N // panel // unroll, steps, tuple(m for b in range(batch) for m in load(0, b)))
    for b in range(batch):
        work[b] = update(N - panel, b)


def pad_rows(row):
    return jnp.broadcast_to(row, (8, N))


def solve_part(
    packed_ref, next_ref, kappa_ref, out_ref,
    work, keep, spread2, spread4, held, coupling, send, recv, send_x, recv_x, zs, send_out, recv_out,
    send_sem, recv_sem, x_sems, send_out_sem, recv_out_sem, *, chunks,
):
    me = lax.axis_index("tm")
    chunk, tile = OWNER.chunk_of(me), OWNER.tile_of(me)
    home, place = me // SPAN, me % SPAN
    levels = chunks.bit_length() - 1
    strides = [2 ** i for i in range(levels)]

    def device(other):
        return (OWNER.device(other, tile), lax.axis_index("obs"))

    def exists(step):
        return jnp.logical_and(chunk + step >= 0, chunk + step < chunks)

    kappa = kappa_ref[pl.ds(tile, 1), :]
    row_id = lax.broadcasted_iota(jnp.int32, (N, N), 0)
    lane_id = lax.broadcasted_iota(jnp.int32, (N, N), 1)
    end = jnp.logical_or(lane_id == 0, lane_id == N - 1)
    degree = jnp.where(end, 1.0, 2.0)
    prior = jnp.where(
        row_id == lane_id, kappa + degree,
        jnp.where(jnp.abs(row_id - lane_id) == 1, -1.0, 0.0),
    )
    weight_row = kappa + degree[:1]
    weight_column = jnp.sum(jnp.where(row_id == lane_id, prior, 0.0), axis=1, keepdims=True)

    def prior_left(m):
        up = jnp.where(row_id == 0, 0.0, pltpu.roll(m, 1, 0))
        down = jnp.where(row_id == N - 1, 0.0, pltpu.roll(m, N - 1, 0))
        return weight_column * m - up - down

    def prior_right(m):
        lanes = lax.broadcasted_iota(jnp.int32, m.shape, 1)
        up = jnp.where(lanes == 0, 0.0, pltpu.roll(m, 1, 1))
        down = jnp.where(lanes == N - 1, 0.0, pltpu.roll(m, N - 1, 1))
        return weight_row * m - up - down

    rates = [packed_ref[i, RATE:RATE + 1, :] for i in range(SPAN)] + [next_ref[:1]]
    first = chunk == 0

    def diagonal(i):
        lead = 1.0
        if i == 0:
            lead = jnp.where(first, 1.0 - rates[0] * rates[0], 1.0)
        return (lead + rates[i + 1] * rates[i + 1]) * prior + unfold(packed_ref[i])

    def side(i):
        return pad_rows(packed_ref[i, SIDE:SIDE + 1, :])

    for b in range(4):
        work[b] = diagonal(2 * b + 1)
    invert(work, 4)
    sides = {i: side(i) for i in range(0, SPAN, 2)}
    after_side = jnp.zeros((8, N), F32)
    for b in range(4):
        i = 2 * b + 1
        inverse = work[b]
        keep[b] = inverse
        middle = prior_right(prior_left(inverse))
        z = dot(side(i), inverse)
        zs[i] = z
        pz = prior_right(z)
        low, high = rates[i], rates[i + 1]
        held[2 * b] = (diagonal(2 * b) if b == 0 else held[2 * b]) - (low * low) * middle
        coupling[b] = (-low * high) * middle
        sides[i - 1] = sides[i - 1] + low * pz
        if b < 3:
            held[2 * b + 2] = diagonal(2 * b + 2) - (high * high) * middle
            sides[i + 1] = sides[i + 1] + high * pz
        else:
            send[0, 0, 0:N, :] = (high * high) * middle
            after_side = after_side - high * pz

    work[0] = held[2]
    work[1] = held[6]
    invert(work, 2)
    for b, i in ((0, 2), (1, 6)):
        wide = jnp.concatenate([coupling[2 * b], coupling[2 * b + 1]], axis=1)
        tall = jnp.concatenate([coupling[2 * b], coupling[2 * b + 1]], axis=0)
        inverse = work[b]
        x = dot(inverse, wide)
        spread2[b] = x
        z = dot(sides[i], inverse)
        zs[i] = z
        vec = dot(z, wide)
        s = dot(tall, x)
        held[i - 2] = held[i - 2] - s[:N, :N]
        sides[i - 2] = sides[i - 2] - vec[:, :N]
        if b == 0:
            held[4] = held[4] - s[N:, N:]
            sides[4] = sides[4] - vec[:, N:]
            coupling[0] = -s[N:, :N]
            coupling[1] = -s[:N, N:]
        else:
            send[0, 0, 0:N, :] += s[N:, N:]
            after_side = after_side + vec[:, N:]
            coupling[2] = -s[:N, N:]
            coupling[3] = -s[N:, :N]

    work[0] = held[4]
    invert(work, 1)
    wide = jnp.concatenate([coupling[0], coupling[2]], axis=1)
    tall = jnp.concatenate([coupling[1], coupling[3]], axis=0)
    inverse = work[0]
    x = dot(inverse, wide)
    spread4[...] = x
    z = dot(sides[4], inverse)
    zs[4] = z
    vec = dot(z, wide)
    s = dot(tall, x)
    right = -s[:N, N:]
    send[0, 0, 0:N, :] += s[N:, N:]
    send[0, 0, N + 8:, :] = s[N:, :N]
    send[0, 0, N:N + 8, :] = after_side + vec[:, N:]

    now, later = pl.ds(0, N + 8), pl.ds(N + 8, N)
    last_stage = len(strides)

    def copy(stage, way, step, part):
        rows = later if part else now
        return pltpu.make_async_remote_copy(
            src_ref=send.at[stage, way, rows], dst_ref=recv.at[stage, way, rows],
            send_sem=send_sem.at[stage, way, part], recv_sem=recv_sem.at[stage, way, part],
            device_id=device(chunk + step), device_id_type=MESH,
        )

    def start(stage, way, step, part):
        @pl.when(exists(step))
        def _():
            copy(stage, way, step, part).start()

    def arrive(stage, way, step, part):
        @pl.when(exists(-step))
        def _():
            copy(stage, way, step, part).wait_recv()

    start(0, 0, 1, 0)
    start(0, 0, 1, 1)
    diag = held[0] - s[:N, :N]
    vector = sides[0] - vec[:, :N]
    arrive(0, 0, 1, 0)
    diag = diag - recv[0, 0, 0:N, :]
    vector = vector - recv[0, 0, N:N + 8, :]

    for stage, stride in enumerate(strides, 1):
        work[0] = diag
        invert(work, 1)
        inverse = work[0]
        z = dot(vector, inverse)
        if stage == 1:
            arrive(0, 0, 1, 1)
        else:
            arrive(stage - 1, 0, stride // 2, 1)
            arrive(stage - 1, 1, -(stride // 2), 1)
            right = -recv[stage - 1, 1, N + 8:, :]
        left = -recv[stage - 1, 0, N + 8:, :]
        wide = jnp.concatenate([left, right], axis=1)
        tall = jnp.concatenate([left.T, right.T], axis=0)
        x = dot(inverse, wide)
        vec = dot(z, wide)
        s = dot(tall, x)
        send[stage, 0, 0:N, :] = s[N:, N:]
        send[stage, 0, N:N + 8, :] = vec[:, N:]
        start(stage, 0, stride, 0)
        send[stage, 1, 0:N, :] = s[:N, :N]
        send[stage, 1, N:N + 8, :] = vec[:, :N]
        start(stage, 1, -stride, 0)
        if stage < last_stage:
            send[stage, 0, N + 8:, :] = s[N:, :N]
            start(stage, 0, stride, 1)
            send[stage, 1, N + 8:, :] = s[:N, N:]
            start(stage, 1, -stride, 1)
        arrive(stage, 0, stride, 0)
        arrive(stage, 1, -stride, 0)
        diag = diag - recv[stage, 0, 0:N, :] - recv[stage, 1, 0:N, :]
        vector = vector - recv[stage, 0, N:N + 8, :] - recv[stage, 1, N:N + 8, :]

    work[0] = diag
    invert(work, 1)
    x0 = dot(vector, work[0])
    send_x[...] = x0

    def copy_x():
        return pltpu.make_async_remote_copy(
            src_ref=send_x, dst_ref=recv_x, send_sem=x_sems.at[0], recv_sem=x_sems.at[1],
            device_id=device(chunk - 1), device_id_type=MESH,
        )

    @pl.when(exists(-1))
    def _():
        copy_x().start()

    @pl.when(exists(1))
    def _():
        copy_x().wait_recv()

    x8 = recv_x[...]
    found = {0: x0, 8: x8}
    last = ((1,), (1,))
    found[4] = zs[4] - dot(jnp.concatenate([x0, x8], axis=1), spread4[...], last)
    for b, i in ((0, 2), (1, 6)):
        found[i] = zs[i] - dot(jnp.concatenate([found[i - 2], found[i + 2]], axis=1), spread2[b], last)
    for b in range(4):
        i = 2 * b + 1
        mixed = rates[i] * found[i - 1] + rates[i + 1] * found[i + 1]
        found[i] = zs[i] + dot(prior_right(mixed), keep[b])
    def copy_out(i):
        return pltpu.make_async_remote_copy(
            src_ref=send_out.at[i], dst_ref=recv_out.at[tile],
            send_sem=send_out_sem.at[i], recv_sem=recv_out_sem.at[tile],
            device_id=(chunk * SPAN + i, lax.axis_index("obs")), device_id_type=MESH,
        )

    def arrive_out(k):
        return pltpu.make_async_remote_copy(
            src_ref=send_out.at[0], dst_ref=recv_out.at[k],
            send_sem=send_out_sem.at[0], recv_sem=recv_out_sem.at[k],
            device_id=(OWNER.device(home, k), lax.axis_index("obs")), device_id_type=MESH,
        )

    for i in range(SPAN):
        send_out[i] = found[i]

        @pl.when(chunk * SPAN + i != me)
        def _():
            copy_out(i).start()

        @pl.when(chunk * SPAN + i == me)
        def _():
            recv_out[tile] = send_out[i]

    for k in range(SPAN):
        @pl.when(OWNER.device(home, k) != me)
        def _():
            arrive_out(k).wait_recv()

        out_ref[:, k * N:(k + 1) * N] = recv_out[k, :1, :]

    for i in range(SPAN):
        @pl.when(chunk * SPAN + i != me)
        def _():
            copy_out(i).wait_send()

    @pl.when(exists(-1))
    def _():
        copy_x().wait_send()

    for part in range(2):
        @pl.when(exists(1))
        def _():
            copy(0, 0, 1, part).wait_send()

        for stage, stride in enumerate(strides, 1):
            if part == 0 or stage < last_stage:
                @pl.when(exists(stride))
                def _():
                    copy(stage, 0, stride, part).wait_send()

                @pl.when(exists(-stride))
                def _():
                    copy(stage, 1, -stride, part).wait_send()


def whole_kernel(
    rows_hbm, label_hbm, prec_hbm, value_hbm, rate_hbm, kappa_hbm, out_ref, *scratch, chunks, peers, parts
):
    for slots in (scratch[parts + 7], scratch[parts + 9]):
        slots[...] = jnp.zeros_like(slots)
    finish = front_part(
        rows_hbm, label_hbm, prec_hbm, value_hbm, rate_hbm, kappa_hbm, *scratch[:parts],
        chunks=chunks, peers=peers,
    )
    kappa, packed, after = scratch[5], scratch[14], scratch[16]
    solve_part(packed, after, kappa, out_ref, *scratch[parts:], chunks=chunks)
    finish()


def posterior(rows, label, prec, value, rate, kappa, chunks, peers):
    total_rows = rows.shape[1]
    stages = chunks.bit_length()
    vmem = pl.BlockSpec(memory_space=pltpu.VMEM)
    hbm = pl.BlockSpec(memory_space=pltpu.HBM)
    dma = pltpu.SemaphoreType.DMA
    front_scratch = [
        pltpu.VMEM((total_rows, N), BF16),
        pltpu.VMEM((1, total_rows), jnp.int32),
        pltpu.VMEM((1, total_rows), F32),
        pltpu.VMEM((1, total_rows), F32),
        pltpu.VMEM(rate.shape, F32),
        pltpu.VMEM(kappa.shape, F32),
        pltpu.VMEM((N, total_rows), BF16),
        pltpu.VMEM((2 * N, total_rows), BF16),
        pltpu.VMEM((2 * N, total_rows), BF16),
        pltpu.VMEM((4 * peers, 2 * N), F32),
        pltpu.VMEM((2, 3, 4, FOLD, N), F32),
        pltpu.VMEM((2, 3, 4, FOLD, N), F32),
        pltpu.VMEM((2, 4, FOLD, N), F32),
        pltpu.VMEM((SPAN, FOLD, N), F32),
        pltpu.VMEM((SPAN, FOLD, N), F32),
        pltpu.VMEM((SPAN, 8, N), F32),
        pltpu.VMEM((8, N), F32),
        dma((5 + total_rows // min(1024, total_rows),)),
        dma((2, 6)),
        dma((2, 6)),
        dma((SPAN,)),
        dma((SPAN,)),
        dma((SPAN,)),
        dma((1,)),
    ]
    solve_scratch = [
        pltpu.VMEM((4, N, N), F32),
        pltpu.VMEM((4, N, N), F32),
        pltpu.VMEM((2, N, 2 * N), F32),
        pltpu.VMEM((N, 2 * N), F32),
        pltpu.VMEM((SPAN, N, N), F32),
        pltpu.VMEM((4, N, N), F32),
        pltpu.VMEM((stages, 2, 2 * N + 8, N), F32),
        pltpu.VMEM((stages, 2, 2 * N + 8, N), F32),
        pltpu.VMEM((8, N), F32),
        pltpu.VMEM((8, N), F32),
        pltpu.VMEM((SPAN, 8, N), F32),
        pltpu.VMEM((SPAN, 8, N), F32),
        pltpu.VMEM((SPAN, 8, N), F32),
        dma((stages, 2, 2)),
        dma((stages, 2, 2)),
        dma((2,)),
        dma((SPAN,)),
        dma((SPAN,)),
    ]
    return pl.pallas_call(
        functools.partial(whole_kernel, chunks=chunks, peers=peers, parts=len(front_scratch)),
        in_specs=[hbm] * 6,
        out_specs=vmem,
        out_shape=jax.ShapeDtypeStruct((1, SPAN * N), F32),
        scratch_shapes=front_scratch + solve_scratch,
        compiler_params=pltpu.CompilerParams(
            collective_id=0, has_side_effects=True, vmem_limit_bytes=64 * 2**20 - 2**16
        ),
        name="posterior",
    )(rows, label, prec, value, rate, kappa)


def on_device(weights, tile_of, obs_prec, obs_value, node_kappa, rate):
    return posterior(
        weights, tile_of, obs_prec, obs_value, rate, node_kappa.reshape(-1, N),
        lax.axis_size("tm") // SPAN, lax.axis_size("obs"),
    )


def solution(mesh):
    placed = (
        P("tm", "obs", None),
        P("tm", "obs"),
        P("tm", "obs"),
        P("tm", "obs"),
        P("obs"),
        P("tm", "obs"),
    )
    return jax.shard_map(
        on_device, mesh=mesh, in_specs=placed, out_specs=P("tm", "obs"), check_vma=False
    )
```

```python
import functools

import jax
import jax.numpy as jnp
from jax import lax
from jax.experimental import pallas as pl
from jax.experimental.pallas import tpu as pltpu
from jax.sharding import PartitionSpec as P

F32 = jnp.float32
BF16 = jnp.bfloat16
N = 128
SPAN = 8
MESH = pl.DeviceIdType.MESH


def dot(left, right, dims=((1,), (0,))):
    return lax.dot_general(
        left, right, (dims, ((), ())), precision=lax.Precision.HIGHEST, preferred_element_type=F32
    )


class Owner:
    def chunk_of(self, me):
        return 2 * (me // 16) + me % 2

    def tile_of(self, me):
        return (me % 16) // 2

    def device(self, chunk, tile):
        return 16 * (chunk // 2) + 2 * tile + chunk % 2


OWNER = Owner()
FOLD = N // 2 + 8
DIAG, SIDE, RATE = N // 2, N // 2 + 1, N // 2 + 2


def fold(block, side):
    half = N // 2
    both = block + block.T
    row = lax.broadcasted_iota(jnp.int32, (half, N), 0)
    lane = lax.broadcasted_iota(jnp.int32, (half, N), 1) - half
    low = both[half:]
    packed = jnp.where((lane >= 0) & (lane <= row), pltpu.roll(both[:half], half, 1), low)
    diag = jnp.sum(jnp.where(lane == row, low, 0.0), axis=0, keepdims=True)
    sub = lax.broadcasted_iota(jnp.int32, (8, N), 0)
    extra = jnp.where(sub == 0, diag, jnp.where(sub == 1, side, 0.0))
    return jnp.concatenate([packed, extra], axis=0)


def unfold(packed):
    half = N // 2
    rows = packed[:half]
    turned = pltpu.roll(rows, half, 1)
    row = lax.broadcasted_iota(jnp.int32, (half, N), 0)
    lane = lax.broadcasted_iota(jnp.int32, (half, N), 1)
    top = jnp.where(lane < row, 0.5 * turned, jnp.where(lane == row, 0.25 * turned, 0.0))
    far = lane - half
    low = jnp.where(
        (far < 0) | (far > row), 0.5 * rows, jnp.where(far == row, 0.25 * packed[half:half + 1], 0.0)
    )
    both = jnp.concatenate([top, low], axis=0)
    return both + both.T


def front_part(
    rows_hbm, label_hbm, prec_hbm, value_hbm, rate_hbm, kappa_hbm,
    rows_ref, label_ref, prec_ref, value_ref, rate_ref, kappa_ref,
    scaled, paired, left, sides, send1, recv1, own, send2, recv2, send3, recv3,
    load_sem, send1_sem, recv1_sem, send2_sem, recv2_sem, send3_sem, recv3_sem,
    *, chunks, peers,
):
    me, x = lax.axis_index("tm"), lax.axis_index("obs")
    plus, minus = lax.rem(x + 1, peers), lax.rem(x + peers - 1, peers)
    far = lax.rem(x + 2, peers)
    chunk, slot = me // SPAN, me % SPAN
    my_chunk, my_tile = OWNER.chunk_of(me), OWNER.tile_of(me)
    total_rows = rows_ref.shape[0]
    block = min(1024, total_rows)
    pairs = sides.shape[0]
    loads = [
        pltpu.make_async_copy(source, target, load_sem.at[i])
        for i, (source, target) in enumerate(
            (
                (label_hbm, label_ref), (prec_hbm, prec_ref), (value_hbm, value_ref),
                (rate_hbm, rate_ref), (kappa_hbm, kappa_ref),
            )
        )
    ]
    row_loads = [
        pltpu.make_async_copy(
            rows_hbm.at[0, pl.ds(i * block, block)], rows_ref.at[pl.ds(i * block, block)], load_sem.at[len(loads) + i]
        )
        for i in range(total_rows // block)
    ]
    for load in loads + row_loads:
        load.start()
    tell = jnp.logical_and(slot == 0, chunk > 0)
    told = my_chunk < chunks - 1

    barrier = pltpu.get_barrier_semaphore()
    awaited = 2
    for other in (plus, minus):
        pl.semaphore_signal(barrier, inc=1, device_id=(me, other), device_id_type=MESH)
    for i in range(SPAN):
        source = my_chunk * SPAN + i

        @pl.when(source != me)
        def _():
            pl.semaphore_signal(barrier, inc=1, device_id=(source, x), device_id_type=MESH)

        awaited = awaited + (OWNER.device(chunk, i) != me).astype(jnp.int32)
        awaited = awaited + jnp.logical_and(tell, OWNER.device(chunk - 1, i) != me).astype(jnp.int32)
    teller = (my_chunk + 1) * SPAN

    @pl.when(jnp.logical_and(told, teller != me))
    def _():
        pl.semaphore_signal(barrier, inc=1, device_id=(teller, x), device_id_type=MESH)

    for stride in [2 ** i for i in range(max(1, chunks.bit_length() - 1))]:
        for other in (my_chunk - stride, my_chunk + stride):
            exists = jnp.logical_and(other >= 0, other < chunks)

            @pl.when(exists)
            def _():
                pl.semaphore_signal(
                    barrier, inc=1, device_id=(OWNER.device(other, my_tile), x), device_id_type=MESH
                )

            awaited = awaited + exists.astype(jnp.int32)
    for i in range(SPAN):
        source = OWNER.device(chunk, i)

        @pl.when(source != me)
        def _():
            pl.semaphore_signal(barrier, inc=1, device_id=(source, x), device_id_type=MESH)

        awaited = awaited + (my_chunk * SPAN + i != me).astype(jnp.int32)

    for load in loads:
        load.wait()
    pair = lax.shift_right_logical(label_ref[...], 1)
    odd = lax.bitwise_and(label_ref[...], 1)
    ones = lambda mask: jnp.where(mask, 1.0, 0.0).astype(BF16)
    for step in range(total_rows // block):
        here = slice(step * block, (step + 1) * block)
        row_loads[step].wait()
        turned = rows_ref[here, :].astype(F32).T
        scaled[:, here] = (turned * prec_ref[:, here]).astype(BF16)
        turned = turned.astype(BF16)
        paired[:N, here] = turned * ones(odd[:, here] == 0)
        paired[N:, here] = turned * ones(odd[:, here] == 1)
    last = (((1,), (1,)), ((), ()))
    part = prec_ref[...] * value_ref[...]
    match = lax.broadcasted_iota(jnp.int32, (pairs, total_rows), 0) == pair
    pieces = []
    for _ in range(3):
        top = part.astype(BF16).astype(F32)
        pieces.append(jnp.where(match, top, 0.0).astype(BF16))
        part = part - top
    side = lax.dot_general(
        jnp.concatenate(pieces, axis=0), paired[...], last, preferred_element_type=F32
    )
    sides[...] = side[:pairs] + side[pairs:2 * pairs] + side[2 * pairs:]

    def copy1(way, stage, q=None):
        piece = (way, stage) if q is None else (way, stage, q)
        sem = stage + (q or 0)
        return pltpu.make_async_remote_copy(
            src_ref=send1.at[piece], dst_ref=recv1.at[piece],
            send_sem=send1_sem.at[way, sem], recv_sem=recv1_sem.at[way, sem],
            device_id=(me, plus if way == 0 else minus), device_id_type=MESH,
        )

    def half(group, part, target, added=()):
        first = 4 * group + 2 * part
        for p in range(2):
            left[p * N:(p + 1) * N, :] = scaled[...] * ones(pair == first + p)
        total = lax.dot_general(left[...], paired[...], last, preferred_element_type=F32)
        for p in range(2):
            side_row = sides[pl.ds(first + p, 1), :]
            for o in range(2):
                q = 2 * p + o
                value = fold(
                    total[p * N:(p + 1) * N, o * N:(o + 1) * N], side_row[:, o * N:(o + 1) * N]
                )
                for way, stage in added:
                    value = value + recv1[way, stage, q]
                target[q] = value

    half(far, 0, send1.at[0, 0])
    half(far, 1, send1.at[1, 0])
    pl.semaphore_wait(barrier, awaited)
    copy1(0, 0).start()
    copy1(1, 0).start()

    def copy3(k):
        return pltpu.make_async_remote_copy(
            src_ref=send3.at[k], dst_ref=recv3, send_sem=send3_sem.at[k], recv_sem=recv3_sem.at[0],
            device_id=(OWNER.device(chunk - 1, k), x), device_id_type=MESH,
        )

    recv3_is_own = jnp.logical_and(told, teller == me)

    @pl.when(jnp.logical_not(told))
    def _():
        recv3[...] = jnp.zeros_like(recv3)

    @pl.when(tell)
    def _():
        for k in range(SPAN):
            send3[k] = full(rate_ref[:, k:k + 1])

            @pl.when(OWNER.device(chunk - 1, k) != me)
            def _():
                copy3(k).start()

    @pl.when(recv3_is_own)
    def _():
        recv3[...] = send3[my_tile]

    half(plus, 1, send1.at[0, 1])
    copy1(0, 1).start()
    half(minus, 0, send1.at[1, 1])
    copy1(1, 1).start()
    copy1(0, 0).wait_recv()
    half(plus, 0, send1.at[0, 2], [(0, 0)])
    for q in range(4):
        copy1(0, 2, q).start()
    copy1(1, 0).wait_recv()
    half(minus, 1, send1.at[1, 2], [(1, 0)])
    for q in range(4):
        copy1(1, 2, q).start()
    half(x, 0, own.at[0])
    half(x, 1, own.at[1])

    sub = lax.broadcasted_iota(jnp.int32, (8, N), 0)

    def copy2(k):
        return pltpu.make_async_remote_copy(
            src_ref=send2.at[k], dst_ref=recv2.at[slot],
            send_sem=send2_sem.at[k], recv_sem=recv2_sem.at[slot],
            device_id=(OWNER.device(chunk, k), x), device_id_type=MESH,
        )

    def arrival(i):
        return pltpu.make_async_remote_copy(
            src_ref=send2.at[0], dst_ref=recv2.at[i], send_sem=send2_sem.at[0], recv_sem=recv2_sem.at[i],
            device_id=(me, plus), device_id_type=MESH,
        )

    copy1(0, 1).wait_recv()
    copy1(1, 1).wait_recv()
    for q in range(4):
        for part in range(2):
            copy1(part, 2, q).wait_recv()
            k = 4 * part + q
            value = own[part, q] + recv1[part, 2, q] + recv1[1 - part, 1, q]
            send2[k, :N // 2] = value[:N // 2]
            send2[k, N // 2:] = jnp.where(sub == 2, full(rate_ref[:, k:k + 1]), value[N // 2:])
            mine = OWNER.device(chunk, k) == me

            @pl.when(jnp.logical_not(mine))
            def _():
                copy2(k).start()

            @pl.when(mine)
            def _():
                recv2[slot] = send2[k]

    for i in range(SPAN):
        @pl.when(my_chunk * SPAN + i != me)
        def _():
            arrival(i).wait_recv()

    @pl.when(jnp.logical_and(told, teller != me))
    def _():
        copy3(0).wait_recv()

    def finish():
        for way in range(2):
            copy1(way, 0).wait_send()
            copy1(way, 1).wait_send()
            for q in range(4):
                copy1(way, 2, q).wait_send()
        for k in range(SPAN):
            @pl.when(OWNER.device(chunk, k) != me)
            def _():
                copy2(k).wait_send()

            @pl.when(jnp.logical_and(tell, OWNER.device(chunk - 1, k) != me))
            def _():
                copy3(k).wait_send()

    return finish


def reciprocal(x):
    r = pltpu.reciprocal(x, approx=True)
    return r * (2.0 - x * r)

def full(x):
    return jnp.broadcast_to(x, (8, N))

def tree_sum(parts):
    while len(parts) > 1:
        parts = [parts[x] + parts[x + 1] for x in range(0, len(parts), 2)]
    return parts[0]


def invert(work, batch, panel=16):
    unroll = 2 if batch <= 2 else 1
    slabs = panel // 8
    lane = lax.broadcasted_iota(jnp.int32, (8, N), 1)
    sub = lax.broadcasted_iota(jnp.int32, (8, N), 0)
    lane_full = lax.broadcasted_iota(jnp.int32, (N, N), 1)
    row_full = lax.broadcasted_iota(jnp.int32, (N, N), 0)
    at = lambda x, s: full(x[s:s + 1, :])

    def load(first, b):
        return [work[b, pl.ds(pl.multiple_of(first + 8 * v, 8), 8), :] for v in range(slabs)]

    def spread(mats, first):
        picks = [jnp.full((8, N), k, jnp.int32) + first for k in range(panel)]
        return [[jnp.take_along_axis(m, pick, axis=1, mode="promise_in_bounds") for m in mats] for pick in picks]

    def update(first, b):
        in_lanes = (lane_full >= first) & (lane_full < first + panel)
        in_rows = (row_full >= first) & (row_full < first + panel)
        old = work[b]
        change = dot(jnp.where(in_lanes & ~in_rows, old, 0.0), old)
        return jnp.where(in_lanes & ~in_rows, 0.0, old) - change

    def step(index, carry):
        first = pl.multiple_of(index * panel, panel)
        after = pl.multiple_of(lax.rem(first + panel, N), panel)
        rows = [[carry[b * slabs + v] for v in range(slabs)] for b in range(batch)]
        columns = [spread(rows[b], first) for b in range(batch)]
        place = lane - first
        inside = (place >= 0) & (place < panel)
        for b in range(batch):
            work[b] = update(first - panel, b)
        coming = [load(after, b) for b in range(batch)]
        below = [spread(coming[b], first) for b in range(batch)]
        for j0 in range(0, panel, 2):
            j1 = j0 + 1
            home, s = j0 // 8, j0 % 8
            pair_lanes = (place == j0) | (place == j1)
            pair_rows = (sub == s) | (sub == s + 1)
            for b in range(batch):
                e, n = columns[b], rows[b]
                p, o, q = at(e[j0][home], s), at(e[j0][home], s + 1), at(e[j1][home], s + 1)
                r = reciprocal(p * q - o * o)
                w00, w01, w11 = q * r, -(o * r), p * r

                m0, m1 = list(e[j0]), list(e[j1])
                m0[home] = jnp.where(sub == s, -1.0, jnp.where(sub == s + 1, 0.0, m0[home]))
                m1[home] = jnp.where(sub == s, 0.0, jnp.where(sub == s + 1, -1.0, m1[home]))
                g0 = [m0[v] * w00 + m1[v] * w01 for v in range(slabs)]
                g1 = [m0[v] * w01 + m1[v] * w11 for v in range(slabs)]
                for k in range(j1 + 1, panel):
                    f0, f1 = at(e[k][home], s), at(e[k][home], s + 1)
                    for v in range(slabs):
                        base = jnp.where(pair_rows, 0.0, e[k][v]) if v == home else e[k][v]
                        e[k][v] = base - (g0[v] * f0 + g1[v] * f1)
                x0 = jnp.where(pair_lanes, jnp.where(place == j0, 1.0, 0.0), at(n[home], s))
                x1 = jnp.where(pair_lanes, jnp.where(place == j1, 1.0, 0.0), at(n[home], s + 1))
                for v in range(slabs):
                    gone = (pair_lanes | pair_rows) if v == home else pair_lanes
                    n[v] = jnp.where(gone, 0.0, n[v]) - (g0[v] * x0 + g1[v] * x1)
        out = []
        for b in range(batch):
            work[b, pl.ds(first, panel), :] = jnp.concatenate(rows[b], axis=0)
            out += [
                jnp.where(inside, 0.0, coming[b][v])
                - tree_sum([below[b][k][v] * at(rows[b][k // 8], k % 8) for k in range(panel)])
                for v in range(slabs)
            ]
        return tuple(out)

    def steps(index, carry):
        for i in range(unroll):
            carry = step(index * unroll + i, carry)
        return carry
    lax.fori_loop(0, N // panel // unroll, steps, tuple(m for b in range(batch) for m in load(0, b)))
    for b in range(batch):
        work[b] = update(N - panel, b)


def pad_rows(row):
    return jnp.broadcast_to(row, (8, N))


def solve_part(
    packed_ref, next_ref, kappa_ref, out_ref,
    work, keep, spread2, spread4, held, coupling, send, recv, send_x, recv_x, zs, send_out, recv_out,
    send_sem, recv_sem, x_sems, send_out_sem, recv_out_sem, *, chunks,
):
    me = lax.axis_index("tm")
    chunk, tile = OWNER.chunk_of(me), OWNER.tile_of(me)
    home, place = me // SPAN, me % SPAN
    levels = chunks.bit_length() - 1
    strides = [2 ** i for i in range(levels)]

    def device(other):
        return (OWNER.device(other, tile), lax.axis_index("obs"))

    def exists(step):
        return jnp.logical_and(chunk + step >= 0, chunk + step < chunks)

    kappa = kappa_ref[pl.ds(tile, 1), :]
    row_id = lax.broadcasted_iota(jnp.int32, (N, N), 0)
    lane_id = lax.broadcasted_iota(jnp.int32, (N, N), 1)
    end = jnp.logical_or(lane_id == 0, lane_id == N - 1)
    degree = jnp.where(end, 1.0, 2.0)
    prior = jnp.where(
        row_id == lane_id, kappa + degree,
        jnp.where(jnp.abs(row_id - lane_id) == 1, -1.0, 0.0),
    )
    weight_row = kappa + degree[:1]
    weight_column = jnp.sum(jnp.where(row_id == lane_id, prior, 0.0), axis=1, keepdims=True)

    def prior_left(m):
        up = jnp.where(row_id == 0, 0.0, pltpu.roll(m, 1, 0))
        down = jnp.where(row_id == N - 1, 0.0, pltpu.roll(m, N - 1, 0))
        return weight_column * m - up - down

    def prior_right(m):
        lanes = lax.broadcasted_iota(jnp.int32, m.shape, 1)
        up = jnp.where(lanes == 0, 0.0, pltpu.roll(m, 1, 1))
        down = jnp.where(lanes == N - 1, 0.0, pltpu.roll(m, N - 1, 1))
        return weight_row * m - up - down

    rates = [packed_ref[i, RATE:RATE + 1, :] for i in range(SPAN)] + [next_ref[:1]]
    first = chunk == 0

    def diagonal(i):
        lead = 1.0
        if i == 0:
            lead = jnp.where(first, 1.0 - rates[0] * rates[0], 1.0)
        return (lead + rates[i + 1] * rates[i + 1]) * prior + unfold(packed_ref[i])

    def side(i):
        return pad_rows(packed_ref[i, SIDE:SIDE + 1, :])

    for b in range(4):
        work[b] = diagonal(2 * b + 1)
    invert(work, 4)
    sides = {i: side(i) for i in range(0, SPAN, 2)}
    after_side = jnp.zeros((8, N), F32)
    for b in range(4):
        i = 2 * b + 1
        inverse = work[b]
        keep[b] = inverse
        middle = prior_right(prior_left(inverse))
        z = dot(side(i), inverse)
        zs[i] = z
        pz = prior_right(z)
        low, high = rates[i], rates[i + 1]
        held[2 * b] = (diagonal(2 * b) if b == 0 else held[2 * b]) - (low * low) * middle
        coupling[b] = (-low * high) * middle
        sides[i - 1] = sides[i - 1] + low * pz
        if b < 3:
            held[2 * b + 2] = diagonal(2 * b + 2) - (high * high) * middle
            sides[i + 1] = sides[i + 1] + high * pz
        else:
            send[0, 0, 0:N, :] = (high * high) * middle
            after_side = after_side - high * pz

    work[0] = held[2]
    work[1] = held[6]
    invert(work, 2)
    for b, i in ((0, 2), (1, 6)):
        wide = jnp.concatenate([coupling[2 * b], coupling[2 * b + 1]], axis=1)
        tall = jnp.concatenate([coupling[2 * b], coupling[2 * b + 1]], axis=0)
        inverse = work[b]
        x = dot(inverse, wide)
        spread2[b] = x
        z = dot(sides[i], inverse)
        zs[i] = z
        vec = dot(z, wide)
        s = dot(tall, x)
        held[i - 2] = held[i - 2] - s[:N, :N]
        sides[i - 2] = sides[i - 2] - vec[:, :N]
        if b == 0:
            held[4] = held[4] - s[N:, N:]
            sides[4] = sides[4] - vec[:, N:]
            coupling[0] = -s[N:, :N]
            coupling[1] = -s[:N, N:]
        else:
            send[0, 0, 0:N, :] += s[N:, N:]
            after_side = after_side + vec[:, N:]
            coupling[2] = -s[:N, N:]
            coupling[3] = -s[N:, :N]

    work[0] = held[4]
    invert(work, 1)
    wide = jnp.concatenate([coupling[0], coupling[2]], axis=1)
    tall = jnp.concatenate([coupling[1], coupling[3]], axis=0)
    inverse = work[0]
    x = dot(inverse, wide)
    spread4[...] = x
    z = dot(sides[4], inverse)
    zs[4] = z
    vec = dot(z, wide)
    s = dot(tall, x)
    right = -s[:N, N:]
    send[0, 0, 0:N, :] += s[N:, N:]
    send[0, 0, N + 8:, :] = s[N:, :N]
    send[0, 0, N:N + 8, :] = after_side + vec[:, N:]

    now, later = pl.ds(0, N + 8), pl.ds(N + 8, N)
    last_stage = len(strides)

    def copy(stage, way, step, part):
        rows = later if part else now
        return pltpu.make_async_remote_copy(
            src_ref=send.at[stage, way, rows], dst_ref=recv.at[stage, way, rows],
            send_sem=send_sem.at[stage, way, part], recv_sem=recv_sem.at[stage, way, part],
            device_id=device(chunk + step), device_id_type=MESH,
        )

    def start(stage, way, step, part):
        @pl.when(exists(step))
        def _():
            copy(stage, way, step, part).start()

    def arrive(stage, way, step, part):
        @pl.when(exists(-step))
        def _():
            copy(stage, way, step, part).wait_recv()

    start(0, 0, 1, 0)
    start(0, 0, 1, 1)
    diag = held[0] - s[:N, :N]
    vector = sides[0] - vec[:, :N]
    arrive(0, 0, 1, 0)
    diag = diag - recv[0, 0, 0:N, :]
    vector = vector - recv[0, 0, N:N + 8, :]

    for stage, stride in enumerate(strides, 1):
        work[0] = diag
        invert(work, 1)
        inverse = work[0]
        z = dot(vector, inverse)
        if stage == 1:
            arrive(0, 0, 1, 1)
        else:
            arrive(stage - 1, 0, stride // 2, 1)
            arrive(stage - 1, 1, -(stride // 2), 1)
            right = -recv[stage - 1, 1, N + 8:, :]
        left = -recv[stage - 1, 0, N + 8:, :]
        wide = jnp.concatenate([left, right], axis=1)
        tall = jnp.concatenate([left.T, right.T], axis=0)
        x = dot(inverse, wide)
        vec = dot(z, wide)
        s = dot(tall, x)
        send[stage, 0, 0:N, :] = s[N:, N:]
        send[stage, 0, N:N + 8, :] = vec[:, N:]
        start(stage, 0, stride, 0)
        send[stage, 1, 0:N, :] = s[:N, :N]
        send[stage, 1, N:N + 8, :] = vec[:, :N]
        start(stage, 1, -stride, 0)
        if stage < last_stage:
            send[stage, 0, N + 8:, :] = s[N:, :N]
            start(stage, 0, stride, 1)
            send[stage, 1, N + 8:, :] = s[:N, N:]
            start(stage, 1, -stride, 1)
        arrive(stage, 0, stride, 0)
        arrive(stage, 1, -stride, 0)
        diag = diag - recv[stage, 0, 0:N, :] - recv[stage, 1, 0:N, :]
        vector = vector - recv[stage, 0, N:N + 8, :] - recv[stage, 1, N:N + 8, :]

    work[0] = diag
    invert(work, 1)
    x0 = dot(vector, work[0])
    send_x[...] = x0

    def copy_x():
        return pltpu.make_async_remote_copy(
            src_ref=send_x, dst_ref=recv_x, send_sem=x_sems.at[0], recv_sem=x_sems.at[1],
            device_id=device(chunk - 1), device_id_type=MESH,
        )

    @pl.when(exists(-1))
    def _():
        copy_x().start()

    @pl.when(exists(1))
    def _():
        copy_x().wait_recv()

    x8 = recv_x[...]
    found = {0: x0, 8: x8}
    last = ((1,), (1,))
    found[4] = zs[4] - dot(jnp.concatenate([x0, x8], axis=1), spread4[...], last)
    for b, i in ((0, 2), (1, 6)):
        found[i] = zs[i] - dot(jnp.concatenate([found[i - 2], found[i + 2]], axis=1), spread2[b], last)
    for b in range(4):
        i = 2 * b + 1
        mixed = rates[i] * found[i - 1] + rates[i + 1] * found[i + 1]
        found[i] = zs[i] + dot(prior_right(mixed), keep[b])
    def copy_out(i):
        return pltpu.make_async_remote_copy(
            src_ref=send_out.at[i], dst_ref=recv_out.at[tile],
            send_sem=send_out_sem.at[i], recv_sem=recv_out_sem.at[tile],
            device_id=(chunk * SPAN + i, lax.axis_index("obs")), device_id_type=MESH,
        )

    def arrive_out(k):
        return pltpu.make_async_remote_copy(
            src_ref=send_out.at[0], dst_ref=recv_out.at[k],
            send_sem=send_out_sem.at[0], recv_sem=recv_out_sem.at[k],
            device_id=(OWNER.device(home, k), lax.axis_index("obs")), device_id_type=MESH,
        )

    for i in range(SPAN):
        send_out[i] = found[i]

        @pl.when(chunk * SPAN + i != me)
        def _():
            copy_out(i).start()

        @pl.when(chunk * SPAN + i == me)
        def _():
            recv_out[tile] = send_out[i]

    for k in range(SPAN):
        @pl.when(OWNER.device(home, k) != me)
        def _():
            arrive_out(k).wait_recv()

        out_ref[:, k * N:(k + 1) * N] = recv_out[k, :1, :]

    for i in range(SPAN):
        @pl.when(chunk * SPAN + i != me)
        def _():
            copy_out(i).wait_send()

    @pl.when(exists(-1))
    def _():
        copy_x().wait_send()

    for part in range(2):
        @pl.when(exists(1))
        def _():
            copy(0, 0, 1, part).wait_send()

        for stage, stride in enumerate(strides, 1):
            if part == 0 or stage < last_stage:
                @pl.when(exists(stride))
                def _():
                    copy(stage, 0, stride, part).wait_send()

                @pl.when(exists(-stride))
                def _():
                    copy(stage, 1, -stride, part).wait_send()


def whole_kernel(
    rows_hbm, label_hbm, prec_hbm, value_hbm, rate_hbm, kappa_hbm, out_ref, *scratch, chunks, peers, parts
):
    for slots in (scratch[parts + 7], scratch[parts + 9]):
        slots[...] = jnp.zeros_like(slots)
    finish = front_part(
        rows_hbm, label_hbm, prec_hbm, value_hbm, rate_hbm, kappa_hbm, *scratch[:parts],
        chunks=chunks, peers=peers,
    )
    kappa, packed, after = scratch[5], scratch[14], scratch[16]
    solve_part(packed, after, kappa, out_ref, *scratch[parts:], chunks=chunks)
    finish()


def posterior(rows, label, prec, value, rate, kappa, chunks, peers):
    total_rows = rows.shape[1]
    stages = chunks.bit_length()
    vmem = pl.BlockSpec(memory_space=pltpu.VMEM)
    hbm = pl.BlockSpec(memory_space=pltpu.HBM)
    dma = pltpu.SemaphoreType.DMA
    front_scratch = [
        pltpu.VMEM((total_rows, N), BF16),
        pltpu.VMEM((1, total_rows), jnp.int32),
        pltpu.VMEM((1, total_rows), F32),
        pltpu.VMEM((1, total_rows), F32),
        pltpu.VMEM(rate.shape, F32),
        pltpu.VMEM(kappa.shape, F32),
        pltpu.VMEM((N, total_rows), BF16),
        pltpu.VMEM((2 * N, total_rows), BF16),
        pltpu.VMEM((2 * N, total_rows), BF16),
        pltpu.VMEM((4 * peers, 2 * N), F32),
        pltpu.VMEM((2, 3, 4, FOLD, N), F32),
        pltpu.VMEM((2, 3, 4, FOLD, N), F32),
        pltpu.VMEM((2, 4, FOLD, N), F32),
        pltpu.VMEM((SPAN, FOLD, N), F32),
        pltpu.VMEM((SPAN, FOLD, N), F32),
        pltpu.VMEM((SPAN, 8, N), F32),
        pltpu.VMEM((8, N), F32),
        dma((5 + total_rows // min(1024, total_rows),)),
        dma((2, 6)),
        dma((2, 6)),
        dma((SPAN,)),
        dma((SPAN,)),
        dma((SPAN,)),
        dma((1,)),
    ]
    solve_scratch = [
        pltpu.VMEM((4, N, N), F32),
        pltpu.VMEM((4, N, N), F32),
        pltpu.VMEM((2, N, 2 * N), F32),
        pltpu.VMEM((N, 2 * N), F32),
        pltpu.VMEM((SPAN, N, N), F32),
        pltpu.VMEM((4, N, N), F32),
        pltpu.VMEM((stages, 2, 2 * N + 8, N), F32),
        pltpu.VMEM((stages, 2, 2 * N + 8, N), F32),
        pltpu.VMEM((8, N), F32),
        pltpu.VMEM((8, N), F32),
        pltpu.VMEM((SPAN, 8, N), F32),
        pltpu.VMEM((SPAN, 8, N), F32),
        pltpu.VMEM((SPAN, 8, N), F32),
        dma((stages, 2, 2)),
        dma((stages, 2, 2)),
        dma((2,)),
        dma((SPAN,)),
        dma((SPAN,)),
    ]
    return pl.pallas_call(
        functools.partial(whole_kernel, chunks=chunks, peers=peers, parts=len(front_scratch)),
        in_specs=[hbm] * 6,
        out_specs=vmem,
        out_shape=jax.ShapeDtypeStruct((1, SPAN * N), F32),
        scratch_shapes=front_scratch + solve_scratch,
        compiler_params=pltpu.CompilerParams(
            collective_id=0, has_side_effects=True, vmem_limit_bytes=64 * 2**20 - 2**16
        ),
        name="posterior",
    )(rows, label, prec, value, rate, kappa)


def on_device(weights, tile_of, obs_prec, obs_value, node_kappa, rate):
    return posterior(
        weights, tile_of, obs_prec, obs_value, rate, node_kappa.reshape(-1, N),
        lax.axis_size("tm") // SPAN, lax.axis_size("obs"),
    )


def solution(mesh):
    placed = (
        P("tm", "obs", None),
        P("tm", "obs"),
        P("tm", "obs"),
        P("tm", "obs"),
        P("obs"),
        P("tm", "obs"),
    )
    return jax.shard_map(
        on_device, mesh=mesh, in_specs=placed, out_specs=P("tm", "obs"), check_vma=False
    )
```
